256 devices in a mesh: dp: 4 (over z_hi, core), ctx: 16 (over x, z_lo), tensor: 4 (over y).
Axes of the slice: x: 4, y: 4, z: 8 (z_hi: 2, z_lo: 4; z = z_hi * 4 + z_lo), core: 2. Of those that a mesh axis runs over, the one named last changes fastest.
Arguments:
- hidden_states: bfloat16 [4, 2048, 8192], P('dp', 'ctx'), may hold values from -6 to 6
- positions: int32 [4, 2048], P('dp', 'ctx'), may hold values from 0 to 2047, as said below
- queries: bfloat16 [4, 2048, 4096], P('dp', 'ctx', 'tensor'), may hold values from -32 to 32
- key_weight: bfloat16 [8192, 512], P('ctx', 'tensor'), may hold values from -0.06641333 to 0.06641333
- value_weight: bfloat16 [8192, 512], P('ctx', 'tensor'), may hold values from -0.0625 to 0.0625
- key_step: float32 [64, 512], P('ctx', 'tensor'), may hold values from 0.003 to 0.01
- value_step: float32 [64, 512], P('ctx', 'tensor'), may hold values from 0.003 to 0.01
- smoothing: float32 [8192], replicated, may hold values from 0.5 to 2
- grad_out: bfloat16 [4, 2048, 4096], P('dp', 'ctx', 'tensor'), may hold values from -6 to 6
Outputs:
- grad_hidden: float32 [4, 2048, 8192], P('dp', 'ctx', 'tensor')
- grad_queries: float32 [4, 2048, 4096], P('dp', 'ctx', 'tensor')
- grad_key_weight: float32 [8192, 512], P('ctx', 'tensor')
- grad_value_weight: float32 [8192, 512], P('ctx', 'tensor')
- grad_key_step: float32 [64, 512], P('ctx', 'tensor')
- grad_value_step: float32 [64, 512], P('ctx', 'tensor')
- grad_smoothing: float32 [8192], replicated
The draws below stay inside these ranges and needn't reach their ends.
Inputs may be any that keep to these rules, and one draw needn't show every extreme that they name: In each sequence positions start at 0 and rise by one from token to token, returning to 0 at the start of each of at most three documents; the first sequence is a single document.
All inputs are finite; a program needn't handle non-finite values.
Results may differ from the reference program's by a relative error of at most 0.029.
The reference program's roundings to bfloat16 on the way count: a program that leaves them out, or rounds other values in their place, can miss the bound.
Values may be sent and summed in bfloat16 or wider, within the bound.
A program may use at most 64 MiB of HBM per device.

```python
import math
import jax
import jax.numpy as jnp
from jax import lax

D = 8192
HD = 128
GQ = 8
GROUP = 128
KVH = 4
QH = 32
LEN = 2048
SEQS = 4


def draw_hidden_states(key, part):
    own_key = jax.random.fold_in(key, 5)
    normals = jax.random.normal(own_key, (SEQS, LEN, D), jnp.float32)
    entries = jnp.clip(normals, -6.0, 6.0)
    return entries.astype(jnp.bfloat16)


def draw_key_weight(key, part):
    own_key = jax.random.fold_in(key, 7)
    normals = jax.random.normal(own_key, (D, KVH * HD), jnp.float32)
    entries = jnp.clip(normals, -6.0, 6.0) * D ** (-0.5)
    return entries.astype(jnp.bfloat16)


def draw_positions(key, part):
    key = jax.random.fold_in(key, 11)
    doc_cuts = jax.random.randint(key, (SEQS, 2), max(LEN // 16, 1), max(LEN // 4, 2))
    first_row = (jnp.arange(SEQS, dtype=jnp.int32) == 0)[:, None]
    doc_cuts = jnp.where(first_row, LEN, doc_cuts).astype(jnp.int32)
    token_index = jnp.arange(LEN, dtype=jnp.int32)[None, :]
    first_start = jnp.where(doc_cuts[:, :1] <= token_index, doc_cuts[:, :1], 0)
    second_start = jnp.where(doc_cuts[:, 1:] <= token_index, doc_cuts[:, 1:], 0)
    return (token_index - jnp.maximum(first_start, second_start)).astype(jnp.int32)


def draw_queries(key, part):
    own_key = jax.random.fold_in(key, 23)
    normal_key = jax.random.fold_in(own_key, 0)
    normals = 3.0 * jax.random.normal(normal_key, (SEQS, LEN, QH, HD), jnp.float32)
    return jnp.clip(normals, -32.0, 32.0).reshape(SEQS, LEN, QH * HD).astype(jnp.bfloat16)


def block_scale(key, extent, shards, smallest, top_value):
    loudness = 1.0
    for dim, parts in shards:
        heights = jax.random.uniform(jax.random.fold_in(jax.random.fold_in(key, 6), dim), (parts,), jnp.float32, smallest / len(shards), top_value / len(shards))
        loudness = loudness * jnp.repeat(jnp.exp(heights), extent[dim] // parts).reshape((-1,) + (1,) * (len(extent) - 1 - dim))
    return loudness


def scatter_about(stream_key, extent, spread, bound, shards=(), kind=jnp.bfloat16):
    array = spread * jax.random.normal(stream_key, extent, jnp.float32)
    if shards:
        array = array * block_scale(stream_key, extent, shards, -0.22, 0.18)
    return jnp.clip(array, -bound, bound).astype(kind)


def setup_inputs(seed: int = 0) -> dict:
    seeds = jax.random.split(jax.random.key(seed), 10)
    hidden_states = draw_hidden_states(jax.random.fold_in(seeds[9], 71), 0)
    positions = draw_positions(jax.random.fold_in(seeds[9], 71), 0)
    queries = draw_queries(jax.random.fold_in(seeds[9], 71), 0)
    key_weight = draw_key_weight(jax.random.fold_in(seeds[9], 71), 0)
    value_weight = scatter_about(seeds[4], (D, KVH * HD), D ** -0.5, 0.0625, ((0, 16), (1, 4)))
    key_step = jnp.clip(jnp.exp(math.log(0.01) - 1.2039728 * jax.random.uniform(seeds[5], (D // GROUP, KVH * HD), jnp.float32) ** block_scale(seeds[5], (D // GROUP, KVH * HD), ((0, 16), (1, 4)), -0.2, 0.2)), 0.003, 0.01)
    value_step = jnp.clip(jnp.exp(math.log(0.01) - 1.2039728 * jax.random.uniform(seeds[6], (D // GROUP, KVH * HD), jnp.float32) ** block_scale(seeds[6], (D // GROUP, KVH * HD), ((0, 16), (1, 4)), -0.2, 0.2)), 0.003, 0.01)
    smoothing = jnp.clip(jnp.exp(jax.random.uniform(seeds[7], (D,), jnp.float32, math.log(0.5), math.log(2.0))), 0.5, 2.0)
    grad_out = scatter_about(seeds[8], (SEQS, LEN, QH * HD), 1.0, 6.0, ((0, 4), (1, 16), (2, 4)))
    return dict(hidden_states=hidden_states, positions=positions, queries=queries, key_weight=key_weight, value_weight=value_weight, key_step=key_step, value_step=value_step, smoothing=smoothing, grad_out=grad_out)


TWO_PI = 2.0 * math.pi


def rope_tables(positions):
    half_size = HD // 2
    frequency = jnp.exp(jnp.arange(half_size, dtype=jnp.float32) * (-2.0 * math.log(10000.0) / HD))
    angles = positions.astype(jnp.float32)[..., None] * frequency
    return jnp.cos(angles), jnp.sin(angles)


def rotate(vectors, cosine, sine_part):
    half_size = vectors.shape[-1] // 2
    lower_half = vectors[..., :half_size]
    upper_half = vectors[..., half_size:]
    return jnp.concatenate([lower_half * cosine - upper_half * sine_part, upper_half * cosine + lower_half * sine_part], axis=-1)


def unrotate(gradient, cosine, sine_part):
    half_size = gradient.shape[-1] // 2
    lower_half = gradient[..., :half_size]
    upper_half = gradient[..., half_size:]
    return jnp.concatenate([lower_half * cosine + upper_half * sine_part, upper_half * cosine - lower_half * sine_part], axis=-1)


def quantize(weight, step_size, smooth_vec):
    step_rows = jnp.repeat(step_size, GROUP, axis=0)
    code_ratio = weight.astype(jnp.float32) * smooth_vec[:, None] / step_rows
    soft_level = code_ratio - jnp.sin(TWO_PI * code_ratio) / TWO_PI
    return (step_rows * soft_level).astype(jnp.bfloat16), code_ratio


def weight_terms(gradient, code_ratio, weight, smooth_vec):
    phase_angle = TWO_PI * code_ratio
    slope_term = 1.0 - jnp.cos(phase_angle)
    grad_weight = gradient * slope_term * smooth_vec[:, None]
    per_entry = gradient * (code_ratio * jnp.cos(phase_angle) - jnp.sin(phase_angle) / TWO_PI)
    grad_step = per_entry.reshape(-1, GROUP, per_entry.shape[1]).sum(axis=1)
    grad_smooth = jnp.sum(gradient * slope_term * weight.astype(jnp.float32), axis=1)
    return grad_weight, grad_step, grad_smooth


def attend(packed):
    query_tile, key_tile, value_tile, dout_tile, offset_tile = packed
    score_scale = HD ** -0.5
    key_order = jnp.arange(LEN, dtype=jnp.int32)
    allowed = (key_order[None, :] <= key_order[:, None]) & (offset_tile[None, :] == offset_tile[:, None])
    scores = jnp.einsum("gqd,kd->gqk", query_tile.astype(jnp.float32), key_tile.astype(jnp.float32)) * score_scale
    masked = jnp.where(allowed[None], scores, -1.0e30)
    row_max = jnp.max(masked, axis=-1, keepdims=True)
    expd = jnp.where(allowed[None], jnp.exp(masked - row_max), 0.0)
    probs = expd / jnp.sum(expd, axis=-1, keepdims=True)
    probs_b = probs.astype(jnp.bfloat16)
    attended = jnp.einsum("gqk,kd->gqd", probs_b.astype(jnp.float32), value_tile.astype(jnp.float32))
    delta_rows = jnp.sum(dout_tile.astype(jnp.float32) * attended, axis=-1, keepdims=True)
    d_probs = jnp.einsum("gqd,kd->gqk", dout_tile.astype(jnp.float32), value_tile.astype(jnp.float32))
    d_scores = (probs * (d_probs - delta_rows)).astype(jnp.bfloat16).astype(jnp.float32)
    query_grad = jnp.einsum("gqk,kd->gqd", d_scores, key_tile.astype(jnp.float32)) * score_scale
    key_grad = jnp.einsum("gqk,gqd->kd", d_scores, query_tile.astype(jnp.float32)) * score_scale
    value_grad = jnp.einsum("gqk,gqd->kd", probs_b.astype(jnp.float32), dout_tile.astype(jnp.float32))
    return query_grad, key_grad, value_grad


def reference(hidden_states, positions, queries, key_weight, value_weight, key_step, value_step, smoothing, grad_out):
    hidden_wide = hidden_states.astype(jnp.float32).reshape(SEQS * LEN, D)
    smoothed = (hidden_wide / smoothing).astype(jnp.bfloat16)
    key_quant, ratio_key = quantize(key_weight, key_step, smoothing)
    value_quant, ratio_value = quantize(value_weight, value_step, smoothing)
    key_raw = jnp.dot(smoothed, key_quant, preferred_element_type=jnp.float32).reshape(SEQS, LEN, KVH, HD)
    values = jnp.dot(smoothed, value_quant, preferred_element_type=jnp.float32).astype(jnp.bfloat16).reshape(SEQS, LEN, KVH, HD)
    cosine, sine_part = rope_tables(positions)
    cosine = cosine[:, :, None, :]
    sine_part = sine_part[:, :, None, :]
    keys = rotate(key_raw, cosine, sine_part).astype(jnp.bfloat16)
    q_rot = rotate(queries.astype(jnp.float32).reshape(SEQS, LEN, QH, HD), cosine, sine_part).astype(jnp.bfloat16)
    offsets = positions - jnp.arange(LEN, dtype=jnp.int32)[None, :]
    q_items = q_rot.reshape(SEQS, LEN, KVH, GQ, HD).transpose(0, 2, 3, 1, 4).reshape(SEQS * KVH, GQ, LEN, HD)
    d_items = grad_out.reshape(SEQS, LEN, KVH, GQ, HD).transpose(0, 2, 3, 1, 4).reshape(SEQS * KVH, GQ, LEN, HD)
    k_items = keys.transpose(0, 2, 1, 3).reshape(SEQS * KVH, LEN, HD)
    v_items = values.transpose(0, 2, 1, 3).reshape(SEQS * KVH, LEN, HD)
    o_items = jnp.repeat(offsets, KVH, axis=0)
    query_grad, key_grad, value_grad = lax.map(attend, (q_items, k_items, v_items, d_items, o_items))
    query_grad = query_grad.reshape(SEQS, KVH, GQ, LEN, HD).transpose(0, 3, 1, 2, 4).reshape(SEQS, LEN, QH, HD)
    grad_queries = unrotate(query_grad, cosine, sine_part).reshape(SEQS, LEN, QH * HD)
    key_grad = key_grad.reshape(SEQS, KVH, LEN, HD).transpose(0, 2, 1, 3)
    key_rounded = unrotate(key_grad, cosine, sine_part).astype(jnp.bfloat16).reshape(SEQS * LEN, KVH * HD)
    value_rounded = value_grad.reshape(SEQS, KVH, LEN, HD).transpose(0, 2, 1, 3).astype(jnp.bfloat16).reshape(SEQS * LEN, KVH * HD)
    d_smoothed = jnp.dot(key_rounded, key_quant.T, preferred_element_type=jnp.float32) + jnp.dot(value_rounded, value_quant.T, preferred_element_type=jnp.float32)
    grad_hidden = (d_smoothed / smoothing).reshape(SEQS, LEN, D)
    grad_kq = jnp.dot(smoothed.T, key_rounded, preferred_element_type=jnp.float32)
    grad_vq = jnp.dot(smoothed.T, value_rounded, preferred_element_type=jnp.float32)
    key_wgrad, key_sgrad, key_smooth = weight_terms(grad_kq, ratio_key, key_weight, smoothing)
    value_wgrad, value_sgrad, value_smooth = weight_terms(grad_vq, ratio_value, value_weight, smoothing)
    grad_smoothing = key_smooth + value_smooth - jnp.sum(d_smoothed * hidden_wide, axis=0) / (smoothing * smoothing)
    return grad_hidden, grad_queries, key_wgrad, value_wgrad, key_sgrad, value_sgrad, grad_smoothing
```

```python
import functools
import math

import jax
import jax.numpy as jnp
from jax import lax
from jax.experimental import pallas as pl
from jax.experimental.pallas import tpu as pltpu
from jax.sharding import PartitionSpec as P

HD = 128
GROUP = 128
TWO_PI = 2.0 * math.pi
LOG2E = 1.4426950408889634
MESH = pl.DeviceIdType.MESH
BF = jnp.bfloat16
F32 = jnp.float32
VM = pl.BlockSpec(memory_space=pltpu.VMEM)
ANY = pl.BlockSpec(memory_space=pl.ANY)
DMA = pltpu.SemaphoreType.DMA


def rope_tables(positions):
    half_size = HD // 2
    frequency = jnp.exp(jnp.arange(half_size, dtype=F32) * (-2.0 * math.log(10000.0) / HD))
    angles = positions.astype(F32)[..., None] * frequency
    cosine, sine = jnp.cos(angles), jnp.sin(angles)
    return (
        jnp.concatenate([cosine, cosine], axis=-1),
        jnp.concatenate([-sine, sine], axis=-1),
    )


class Place:
    def __init__(self):
        self.ctx = lax.axis_index("ctx")
        self.dp = lax.axis_index("dp")
        self.y = lax.axis_index("tensor")
        self.x = lax.div(self.ctx, 4)
        self.zl = lax.rem(self.ctx, 4)
        self.zh = lax.div(self.dp, 2)
        self.c = lax.rem(self.dp, 2)
        self.z = self.zh * 4 + self.zl

    def xn(self, d):
        return {"ctx": lax.rem(self.x + (d + 4), 4) * 4 + self.zl, "dp": self.dp}

    def zn(self, d):
        z = lax.rem(self.z + (d + 8), 8)
        return {"ctx": self.x * 4 + lax.rem(z, 4), "dp": lax.div(z, 4) * 2 + self.c}

    def zline(self, d):
        return {"ctx": self.x * 4 + lax.rem(self.zl + d, 4), "dp": self.dp}

    def yn(self, d):
        return {"tensor": lax.rem(self.y + (d + 4), 4)}

    def sib(self):
        return {"dp": self.zh * 2 + (1 - self.c)}

    def far(self, other):
        c = (1 - self.c) if other else self.c
        return {"dp": (1 - self.zh) * 2 + c}

    def mix(self, first, second):
        c = self.c
        return {k: first[k] * (1 - c) + second[k] * c for k in first}


def greet(peers):
    barrier = pltpu.get_barrier_semaphore()
    for peer in peers:
        pl.semaphore_signal(barrier, inc=1, device_id=peer, device_id_type=MESH)
    pl.semaphore_wait(barrier, len(peers))


class Sender:
    def __init__(self, sems):
        self.sems = sems
        self.used = 0
        self.copies = []

    def __call__(self, src, dst, recv, peer):
        copy = pltpu.make_async_remote_copy(
            src_ref=src,
            dst_ref=dst,
            send_sem=self.sems.at[self.used],
            recv_sem=recv,
            device_id=peer,
            device_id_type=MESH,
        )
        self.used += 1
        copy.start()
        self.copies.append(copy)

    def drain(self):
        for copy in self.copies:
            copy.wait_send()
        self.copies = []


def arrived(ref, sem):
    pltpu.make_async_copy(ref, ref, sem).wait()


def proj_kernel(
    part, hid, smooth, cos, sin,
    w_out, smt_out, kv,
    wbuf, sm, smt, acc,
    ssem, nsem, sibsem, zsem, xsem, csem,
):
    p = Place()
    c = p.c
    a0 = p.x * (1 - c) + p.zl * c
    b0 = p.zl * (1 - c) + p.x * c

    def slot(a, b):
        a = lax.rem(a0 + (a + 4), 4)
        b = lax.rem(b0 + (b + 4), 4)
        return (a * 4 + b) * (1 - c) + (b * 4 + a) * c

    an = {d: p.mix(p.xn(d), p.zn(d)) for d in (1, -1)}
    bn = {d: p.mix(p.zn(d), p.xn(d)) for d in (1, -1)}
    sib = p.sib()
    greet([an[1], an[-1], bn[1], bn[-1], sib] + [p.zline(k) for k in (1, 2, 3)])
    send = Sender(ssem)

    def chunk(s, sub):
        return wbuf.at[s * 4 + c * 2 + sub]

    def net(s, sub, peer):
        send(chunk(s, sub), chunk(s, sub), nsem.at[s * 2 + sub], peer)

    def got(s, sub):
        arrived(chunk(s, sub), nsem.at[s * 2 + sub])

    def to_sib(s):
        ref = wbuf.at[pl.ds(s * 4 + c * 2, 2)]
        send(ref, ref, sibsem.at[s], sib)

    def from_sib(s):
        arrived(wbuf.at[pl.ds(s * 4 + (1 - c) * 2, 2)], sibsem.at[s])

    def dot(s, h):
        w = wbuf[pl.ds(s * 4 + h * 2, 2)].reshape(256, 256)
        acc[...] += jnp.dot(sm[s * 2 + h], w, preferred_element_type=F32)

    own = slot(0, 0)
    wbuf[pl.ds(own * 4, 4)] = part[...]
    for sub in (0, 1):
        net(own, sub, an[1])
        net(own, 1 - sub, an[-1])
        net(own, sub, bn[1])
        net(own, 1 - sub, bn[-1])

    inverse = 1.0 / smooth[...]
    for j in range(32):
        cols = slice(j * 256, (j + 1) * 256)
        block = (hid[:, cols].astype(F32) * inverse[:, cols])
        sm[j] = block.astype(BF)
        smt[j] = block.T.astype(BF)
    smt_copy = pltpu.make_async_copy(smt, smt_out, csem.at[0])
    smt_copy.start()
    acc[...] = jnp.zeros_like(acc)
    dot(own, 0)
    dot(own, 1)

    left, right, far = slot(-1, 0), slot(1, 0), slot(2, 0)
    got(left, 0)
    net(left, 0, an[1])
    got(right, 1)
    net(right, 1, an[-1])
    for s, sub in ((left, 0), (right, 1)):
        net(s, sub, bn[1])
        net(s, sub, bn[-1])
    for s, sub in ((left, 1), (right, 0)):
        got(s, sub)
        net(s, sub, bn[1])
        net(s, sub, bn[-1])
        to_sib(s)

    def across(a):
        bl, br = slot(a, -1), slot(a, 1)
        got(bl, 0)
        net(bl, 0, bn[1])
        got(br, 1)
        net(br, 1, bn[-1])
        got(bl, 1)
        got(br, 0)
        to_sib(bl)
        to_sib(br)
        dot(bl, c)
        dot(br, c)

    across(0)
    dot(left, c)
    dot(right, c)
    for sub in (0, 1):
        got(far, sub)
        net(far, sub, bn[1])
        net(far, sub, bn[-1])
    to_sib(far)
    dot(far, c)
    for a in (-1, 1, 2):
        across(a)
    order = [(0, -1), (0, 1)]
    for a in (0, -1, 1, 2):
        s = slot(a, 2)
        got(s, 0)
        got(s, 1)
        to_sib(s)
        dot(s, c)
    for a in (-1, 1, 0, 2):
        for b in (0, -1, 1, 2):
            if a == 0 and b == 0:
                continue
            s = slot(b, a)
            from_sib(s)
            dot(s, 1 - c)

    w_copy = pltpu.make_async_copy(wbuf, w_out, csem.at[1])
    w_copy.start()

    key_raw = acc[:, :HD]
    rotated = key_raw * cos[...] + pltpu.roll(key_raw, HD // 2, 1) * sin[...]
    kv[p.ctx, :, :HD] = rotated.astype(BF)
    kv[p.ctx, :, HD:] = acc[:, HD:].astype(BF)
    for k in (2, 1, 3):
        send(kv.at[p.ctx], kv.at[p.ctx], zsem.at[k - 1], p.zline(k))
    for k in (1, 3, 2):
        arrived(kv.at[p.x * 4 + lax.rem(p.zl + (4 - k), 4)], zsem.at[k - 1])

    def half(d, h):
        return kv.at[pl.ds(lax.rem(p.x + (d + 4), 4) * 4 + h * 2, 2)]

    def xsend(d, h, dirn, which):
        send(half(d, h), half(d, h), xsem.at[which], p.xn(dirn))

    xsend(0, 0, 1, 0)
    xsend(0, 1, -1, 3)
    xsend(0, 1, 1, 1)
    xsend(0, 0, -1, 2)
    arrived(half(-1, 0), xsem.at[0])
    xsend(-1, 0, 1, 4)
    arrived(half(1, 1), xsem.at[3])
    xsend(1, 1, -1, 5)
    arrived(half(-1, 1), xsem.at[1])
    arrived(half(1, 0), xsem.at[2])
    arrived(half(2, 0), xsem.at[4])
    arrived(half(2, 1), xsem.at[5])
    send.drain()
    smt_copy.wait()
    w_copy.wait()


def project(part, hid, smooth, cos, sin):
    return pl.pallas_call(
        proj_kernel,
        name="proj",
        out_shape=(
            jax.ShapeDtypeStruct((64, 128, 256), BF),
            jax.ShapeDtypeStruct((32, 256, 128), BF),
            jax.ShapeDtypeStruct((16, 128, 256), BF),
        ),
        in_specs=[VM] * 5,
        out_specs=(ANY, ANY, VM),
        scratch_shapes=[
            pltpu.VMEM((64, 128, 256), BF),
            pltpu.VMEM((32, 128, 256), BF),
            pltpu.VMEM((32, 256, 128), BF),
            pltpu.VMEM((128, 256), F32),
            DMA((64,)),
            DMA((32,)),
            DMA((16,)),
            DMA((3,)),
            DMA((6,)),
            DMA((2,)),
        ],
        compiler_params=pltpu.CompilerParams(
            collective_id=0, has_side_effects=True, vmem_limit_bytes=40 << 20
        ),
    )(part, hid, smooth, cos, sin)


def attn_kernel(
    kv, queries, dout, start, cos, sin, dkv, gq, qr, qt, do, dot_t, scr, dpr, dq
):
    ctx = lax.axis_index("ctx")
    groups = qr.shape[0] // 128
    scale = HD ** (-0.5)
    for g in range(groups):
        cols = slice(g * 128, (g + 1) * 128)
        q = queries[:, cols].astype(F32)
        q = (q * cos[...] + pltpu.roll(q, HD // 2, 1) * sin[...]).astype(BF)
        qr[cols, :] = q
        qt[:, cols] = q.astype(F32).T.astype(BF)
        d = dout[:, cols]
        do[cols, :] = d
        dot_t[:, cols] = d.astype(F32).T.astype(BF)
    width = 256
    chunks = qr.shape[0] // width
    q_index = ctx * 128 + lax.rem(lax.broadcasted_iota(jnp.int32, (1, width), 1), 128)
    first = start[:, :width]
    row = lax.broadcasted_iota(jnp.int32, (128, width), 0)

    def stats(j, carry):
        kj = kv[j, :, :HD]
        vj = kv[j, :, HD:]
        k_index = row + j * 128
        allowed = (k_index <= q_index) & (k_index >= first)
        out = []
        for n in range(chunks):
            cols = slice(n * width, (n + 1) * width)
            m, l, u = carry[n]
            s = jnp.dot(kj, qt[:, cols], preferred_element_type=F32) * (scale * LOG2E)
            s = jnp.where(allowed, s, -1e30)
            d = jnp.dot(vj, dot_t[:, cols], preferred_element_type=F32)
            scr[j, :, cols] = s
            dpr[j, :, cols] = d
            m_new = jnp.maximum(m, jnp.max(s, axis=0, keepdims=True))
            e = jnp.where(allowed, jnp.exp2(s - m_new), 0.0)
            fix = jnp.exp2(m - m_new)
            l = l * fix + jnp.sum(e, axis=0, keepdims=True)
            u = u * fix + jnp.sum(e * d, axis=0, keepdims=True)
            out.append((m_new, l, u))
        return tuple(out)

    zero = jnp.zeros((1, width), F32)
    carry = lax.fori_loop(
        0, ctx + 1, stats, tuple((zero - 1e30, zero, zero) for _ in range(chunks))
    )
    shift = [m + jnp.log2(l) for m, l, u in carry]
    delta = [u / l for m, l, u in carry]
    dq[...] = jnp.zeros_like(dq)

    def grads(j, _):
        kt = kv[j, :, :HD].astype(F32).T.astype(BF)
        dk = jnp.zeros((128, HD), F32)
        dv = jnp.zeros((128, HD), F32)
        for n in range(chunks):
            cols = slice(n * width, (n + 1) * width)
            prob = jnp.exp2(scr[j, :, cols] - shift[n])
            ds = (prob * (dpr[j, :, cols] - delta[n])).astype(BF)
            dv += jnp.dot(prob.astype(BF), do[cols, :], preferred_element_type=F32)
            dk += jnp.dot(ds, qr[cols, :], preferred_element_type=F32)
            dq[:, cols] += jnp.dot(kt, ds, preferred_element_type=F32)
        dkv[j, :, :HD] = (dk * scale).astype(BF)
        dkv[j, :, HD:] = dv.astype(BF)
        return 0

    lax.fori_loop(0, ctx + 1, grads, 0)

    def clear(j, _):
        dkv[j] = jnp.zeros((128, 2 * HD), BF)
        return 0

    lax.fori_loop(ctx + 1, 16, clear, 0)
    for g in range(groups):
        cols = slice(g * 128, (g + 1) * 128)
        t = dq[:, cols].T * scale
        gq[:, cols] = t * cos[...] - pltpu.roll(t, HD // 2, 1) * sin[...]


def attend(kv, queries, dout, start, cos, sin):
    rows = queries.shape[1]
    return pl.pallas_call(
        attn_kernel,
        name="attn",
        out_shape=(
            jax.ShapeDtypeStruct((16, 128, 256), BF),
            jax.ShapeDtypeStruct((128, rows), F32),
        ),
        in_specs=[VM] * 6,
        out_specs=(VM, VM),
        scratch_shapes=[
            pltpu.VMEM((rows, HD), BF),
            pltpu.VMEM((HD, rows), BF),
            pltpu.VMEM((rows, HD), BF),
            pltpu.VMEM((HD, rows), BF),
            pltpu.VMEM((16, 128, rows), F32),
            pltpu.VMEM((16, 128, rows), F32),
            pltpu.VMEM((HD, rows), F32),
        ],
        compiler_params=pltpu.CompilerParams(vmem_limit_bytes=48 << 20),
    )(kv, queries, dout, start, cos, sin)


def grad_kernel(
    dkv, cos, sin, w_hbm, smt_hbm, ss_hbm, st_hbm, cb_hbm,
    dcol, gkw, gvw, steps, gsm,
    w, smt, ss, st, cb,
    a_r1, a_r2, a_st, a_t, a_zs, a_z,
    hs, hr, ms, r1, r2, sx, tz, zs, zr, fb,
    y_s, y_r1, y_r2, yv, gs,
    ssem, csem, a1sem, a2sem, azsem, hsem, r1sem, r2sem, zsem, fsem,
    y1sem, y2sem, vsem, gxsem, gzsem,
):
    p = Place()
    c = p.c
    loads = [
        pltpu.make_async_copy(s, d, csem.at[i])
        for i, (s, d) in enumerate(
            ((smt_hbm, smt), (w_hbm, w), (ss_hbm, ss), (st_hbm, st), (cb_hbm, cb))
        )
    ]
    for load in loads:
        load.start()
    xr, xl = p.xn(1), p.xn(-1)
    yr, yl = p.yn(1), p.yn(-1)
    sib = p.sib()
    greet(
        [xr, xl, p.xn(2), yr, yl, p.yn(2), sib, p.far(1)] + [p.zn(k) for k in range(1, 8)]
    )
    send = Sender(ssem)

    def xblk(d):
        return lax.rem(p.x + (d + 4), 4)

    def ahalf(d, h):
        return pl.ds(xblk(d) * 4 + h * 2, 2)

    send(dkv.at[ahalf(2, 0)], a_r1.at[0], a1sem.at[0], xr)
    send(dkv.at[ahalf(2, 1)], a_r1.at[1], a1sem.at[1], xl)
    send(dkv.at[ahalf(1, 1)], a_r2.at[0, 1], a2sem.at[1], xr)
    send(dkv.at[ahalf(-1, 0)], a_r2.at[1, 0], a2sem.at[2], xl)
    arrived(a_r1.at[0], a1sem.at[0])
    a_st[0] = (dkv[ahalf(1, 0)].astype(F32) + a_r1[0].astype(F32)).astype(BF)
    send(a_st.at[0], a_r2.at[0, 0], a2sem.at[0], xr)
    arrived(a_r1.at[1], a1sem.at[1])
    a_st[1] = (dkv[ahalf(-1, 1)].astype(F32) + a_r1[1].astype(F32)).astype(BF)
    send(a_st.at[1], a_r2.at[1, 1], a2sem.at[3], xl)
    for i, (s, h) in ((1, (0, 1)), (2, (1, 0)), (0, (0, 0)), (3, (1, 1))):
        arrived(a_r2.at[s, h], a2sem.at[i])
    for h in (0, 1):
        total = (
            dkv[ahalf(0, h)].astype(F32) + a_r2[0, h].astype(F32) + a_r2[1, h].astype(F32)
        )
        a_t[h * 2 : h * 2 + 2] = total
        a_zs[h * 2 : h * 2 + 2] = total.astype(BF)
    for k in (2, 1, 3):
        send(a_zs.at[lax.rem(p.zl + k, 4)], a_z.at[k - 1], azsem.at[k - 1], p.zline(k))
    d_kv = a_t[p.zl]
    for k in (1, 3, 2):
        arrived(a_z.at[k - 1], azsem.at[k - 1])
        d_kv += a_z[k - 1].astype(F32)
    dk = d_kv[:, :HD]
    dk = dk * cos[...] - pltpu.roll(dk, HD // 2, 1) * sin[...]
    g = jnp.concatenate([dk, d_kv[:, HD:]], axis=1).astype(BF)

    dirs = (2, 1, -1, 0)

    def wgrad(k):
        blk = xblk(dirs[k])
        for zl in range(4):
            j = (blk * 4 + zl) * 2
            hs[k, zl] = jnp.dot(smt[j + (1 - c)], g, preferred_element_type=F32).astype(BF)
            ms[k, zl] = jnp.dot(smt[j + c], g, preferred_element_type=F32).astype(BF)
        send(hs.at[k], hr.at[k], hsem.at[k], sib)

    def pair(k, h):
        part = slice(h * 2, h * 2 + 2)
        return ms[k, part].astype(F32) + hr[k, part].astype(F32)

    def dgrad(d, h):
        blk = lax.rem(p.y + (d + 4), 4) * 16 + h * 8
        out = []
        for i in range(4):
            wb = w[pl.ds(blk + i * 2, 2)].reshape(256, 256)
            out.append(
                lax.dot_general(g, wb, (((1,), (1,)), ((), ())), preferred_element_type=F32)
            )
        return out

    def dstore(k, d, h, extra=None):
        for i, piece in enumerate(dgrad(d, h)):
            cols = slice(i * 256, (i + 1) * 256)
            if extra is not None:
                piece = piece + extra[:, cols].astype(F32)
            y_s[k, h, :, cols] = piece.astype(BF)

    loads[0].wait()
    wgrad(0)
    loads[1].wait()
    dstore(0, 2, 0)
    send(y_s.at[0, 0], y_r1.at[0], y1sem.at[0], yr)
    dstore(0, 2, 1)
    send(y_s.at[0, 1], y_r1.at[1], y1sem.at[1], yl)
    wgrad(1)
    arrived(hr.at[0], hsem.at[0])
    for h in (0, 1):
        sx[0, h] = pair(0, h).astype(BF)
        send(sx.at[0, h], r1.at[h], r1sem.at[h], (xr, xl)[h])
    dstore(1, 1, 1)
    send(y_s.at[1, 1], y_r2.at[0, 1], y2sem.at[1], yr)
    dstore(2, -1, 0)
    send(y_s.at[2, 0], y_r2.at[1, 0], y2sem.at[2], yl)
    wgrad(2)
    arrived(hr.at[1], hsem.at[1])
    sx[1, 1] = pair(1, 1).astype(BF)
    send(sx.at[1, 1], r2.at[0, 1], r2sem.at[1], xr)
    arrived(hr.at[2], hsem.at[2])
    sx[2, 0] = pair(2, 0).astype(BF)
    send(sx.at[2, 0], r2.at[1, 0], r2sem.at[2], xl)
    wgrad(3)
    arrived(y_r1.at[0], y1sem.at[0])
    dstore(1, 1, 0, y_r1.at[0])
    send(y_s.at[1, 0], y_r2.at[0, 0], y2sem.at[0], yr)
    arrived(y_r1.at[1], y1sem.at[1])
    dstore(2, -1, 1, y_r1.at[1])
    send(y_s.at[2, 1], y_r2.at[1, 1], y2sem.at[3], yl)
    arrived(r1.at[0], r1sem.at[0])
    sx[1, 0] = (pair(1, 0) + r1[0].astype(F32)).astype(BF)
    send(sx.at[1, 0], r2.at[0, 0], r2sem.at[0], xr)
    arrived(r1.at[1], r1sem.at[1])
    sx[2, 1] = (pair(2, 1) + r1[1].astype(F32)).astype(BF)
    send(sx.at[2, 1], r2.at[1, 1], r2sem.at[3], xl)
    for h in (0, 1):
        for i, piece in enumerate(dgrad(0, h)):
            dcol[:, h * 1024 + i * 256 : h * 1024 + (i + 1) * 256] = piece

    arrived(hr.at[3], hsem.at[3])
    for i, (s, h) in ((1, (0, 1)), (2, (1, 0)), (0, (0, 0)), (3, (1, 1))):
        arrived(r2.at[s, h], r2sem.at[i])
    for h in (0, 1):
        total = pair(3, h) + r2[0, h].astype(F32) + r2[1, h].astype(F32)
        total = total.reshape(4, 128, 256)
        tz[h * 4 : h * 4 + 4] = total
        zs[h * 4 : h * 4 + 4] = total.astype(BF)
    for k in (4, 3, 5, 2, 6, 1, 7):
        z = lax.rem(p.z + k, 8)
        send(zs.at[lax.rem(z, 4) * 2 + lax.div(z, 4)], zr.at[k - 1], zsem.at[k - 1], p.zn(k))

    for i, (s, h) in ((1, (0, 1)), (2, (1, 0)), (0, (0, 0)), (3, (1, 1))):
        arrived(y_r2.at[s, h], y2sem.at[i])
    for h in (0, 1):
        cols = slice(h * 1024, (h + 1) * 1024)
        dcol[:, cols] += y_r2[0, h].astype(F32) + y_r2[1, h].astype(F32)

    f = tz[p.zl * 2 + p.zh]
    for k in (1, 7, 2, 6, 3, 5, 4):
        arrived(zr.at[k - 1], zsem.at[k - 1])
        f += zr[k - 1].astype(F32)
    mine = c * 2 + p.zh
    fb[mine] = f.astype(BF)
    for i, peer in ((0, p.far(0)), (1, p.far(1)), (2, sib)):
        send(fb.at[mine], fb.at[mine], fsem.at[i], peer)
    for load in loads[2:]:
        load.wait()
    arrived(fb.at[(1 - c) * 2 + p.zh], fsem.at[2])
    arrived(fb.at[c * 2 + (1 - p.zh)], fsem.at[0])
    arrived(fb.at[(1 - c) * 2 + (1 - p.zh)], fsem.at[1])
    vec = []
    for q in range(4):
        rows = slice(q * 128, (q + 1) * 128)
        f = fb[q].astype(F32)
        t = f * cb[rows, :]
        t = t[:, :HD] + t[:, HD:]
        vec.append(jnp.sum(t.T, axis=0, keepdims=True))
    yv[p.y] = jnp.concatenate(vec + vec, axis=0)
    for k in (2, 1, 3):
        send(yv.at[p.y], yv.at[p.y], vsem.at[k - 1], p.yn(k))
    for q in range(4):
        rows = slice(q * 128, (q + 1) * 128)
        f = fb[q].astype(F32)
        o = f * ss[rows, :]
        gkw[rows, :] = o[:, :HD]
        gvw[rows, :] = o[:, HD:]
        steps[q : q + 1, :] = jnp.sum(f * st[rows, :], axis=0, keepdims=True)
    for k in (1, 3, 2):
        arrived(yv.at[lax.rem(p.y + (4 - k), 4)], vsem.at[k - 1])
    own = p.zl * 4 + p.x
    gs[own] = (yv[0] + yv[1]) + (yv[2] + yv[3])
    for k in (2, 1, 3):
        send(gs.at[own], gs.at[own], gxsem.at[k - 1], p.xn(k))
    for k in (1, 3, 2):
        arrived(gs.at[p.zl * 4 + lax.rem(p.x + (4 - k), 4)], gxsem.at[k - 1])
    for k in (2, 1, 3):
        row = pl.ds(p.zl * 4, 4)
        send(gs.at[row], gs.at[row], gzsem.at[k - 1], p.zline(k))
    for k in (1, 3, 2):
        arrived(gs.at[pl.ds(lax.rem(p.zl + (4 - k), 4) * 4, 4)], gzsem.at[k - 1])
    for i in range(16):
        gsm[i * 4 : i * 4 + 4, :] = gs[(i % 4) * 4 + i // 4, :4, :]
    send.drain()


def gradients(dkv, cos, sin, w, smt, ss, st, cb):
    return pl.pallas_call(
        grad_kernel,
        name="grads",
        out_shape=(
            jax.ShapeDtypeStruct((128, 2048), F32),
            jax.ShapeDtypeStruct((512, 128), F32),
            jax.ShapeDtypeStruct((512, 128), F32),
            jax.ShapeDtypeStruct((4, 256), F32),
            jax.ShapeDtypeStruct((64, 128), F32),
        ),
        in_specs=[VM] * 3 + [ANY] * 5,
        out_specs=(VM,) * 5,
        scratch_shapes=[
            pltpu.VMEM((64, 128, 256), BF),
            pltpu.VMEM((32, 256, 128), BF),
            pltpu.VMEM((512, 256), F32),
            pltpu.VMEM((512, 256), F32),
            pltpu.VMEM((512, 256), F32),
            pltpu.VMEM((2, 2, 128, 256), BF),
            pltpu.VMEM((2, 2, 2, 128, 256), BF),
            pltpu.VMEM((2, 2, 128, 256), BF),
            pltpu.VMEM((4, 128, 256), F32),
            pltpu.VMEM((4, 128, 256), BF),
            pltpu.VMEM((3, 128, 256), BF),
            pltpu.VMEM((4, 4, 256, 256), BF),
            pltpu.VMEM((4, 4, 256, 256), BF),
            pltpu.VMEM((4, 4, 256, 256), BF),
            pltpu.VMEM((2, 2, 256, 256), BF),
            pltpu.VMEM((2, 2, 2, 256, 256), BF),
            pltpu.VMEM((3, 2, 2, 256, 256), BF),
            pltpu.VMEM((8, 128, 256), F32),
            pltpu.VMEM((8, 128, 256), BF),
            pltpu.VMEM((7, 128, 256), BF),
            pltpu.VMEM((4, 128, 256), BF),
            pltpu.VMEM((3, 2, 128, 1024), BF),
            pltpu.VMEM((2, 128, 1024), BF),
            pltpu.VMEM((2, 2, 128, 1024), BF),
            pltpu.VMEM((4, 8, 128), F32),
            pltpu.VMEM((16, 8, 128), F32),
            DMA((48,)),
            DMA((5,)),
            DMA((2,)),
            DMA((4,)),
            DMA((3,)),
            DMA((4,)),
            DMA((2,)),
            DMA((4,)),
            DMA((7,)),
            DMA((3,)),
            DMA((2,)),
            DMA((4,)),
            DMA((3,)),
            DMA((3,)),
            DMA((3,)),
        ],
        compiler_params=pltpu.CompilerParams(
            collective_id=1, has_side_effects=True, vmem_limit_bytes=56 << 20
        ),
    )(dkv, cos, sin, w, smt, ss, st, cb)


def body(
    hidden_states,
    positions,
    queries,
    key_weight,
    value_weight,
    key_step,
    value_step,
    smoothing,
    grad_out,
):
    shard_index = lax.axis_index("ctx")
    shard_rows = key_weight.shape[0]
    smooth_rows = lax.dynamic_slice_in_dim(smoothing, shard_index * shard_rows, shard_rows)
    weight = jnp.concatenate([key_weight, value_weight], axis=1).astype(F32)
    step = jnp.repeat(jnp.concatenate([key_step, value_step], axis=1), GROUP, axis=0)
    ratio = weight * smooth_rows[:, None] / step
    phase = TWO_PI * ratio
    sine = jnp.sin(phase) / TWO_PI
    cosine = jnp.cos(phase)
    quant = (step * (ratio - sine)).astype(BF)
    slope = 1.0 - cosine
    ss = slope * smooth_rows[:, None]
    st = ratio * cosine - sine
    cb = slope * weight - quant.astype(F32) / smooth_rows[:, None]

    cos, sin = rope_tables(positions[0])
    w, smt, kv = project(
        quant.reshape(4, 128, 256), hidden_states[0], smoothing[None, :], cos, sin
    )
    tok = positions.shape[1]
    start = shard_index * tok + jnp.arange(tok, dtype=jnp.int32) - positions[0]
    start = jnp.tile(start, queries.shape[2] // HD)[None, :]
    dkv, gq = attend(kv, queries[0], grad_out[0], start, cos, sin)
    dcol, gkw, gvw, steps, gsm = gradients(dkv, cos, sin, w, smt, ss, st, cb)
    width = dcol.shape[1]
    smooth_cols = lax.dynamic_slice_in_dim(smoothing, lax.axis_index("tensor") * width, width)
    grad_hidden = (dcol / smooth_cols)[None]
    return (
        grad_hidden,
        gq[None],
        gkw,
        gvw,
        steps[:, :HD],
        steps[:, HD:],
        gsm.reshape(smoothing.shape),
    )


def solution(mesh):
    in_specs = (
        P("dp", "ctx", None),
        P("dp", "ctx"),
        P("dp", "ctx", "tensor"),
        P("ctx", "tensor"),
        P("ctx", "tensor"),
        P("ctx", "tensor"),
        P("ctx", "tensor"),
        P(),
        P("dp", "ctx", "tensor"),
    )
    out_specs = (
        P("dp", "ctx", "tensor"),
        P("dp", "ctx", "tensor"),
        P("ctx", "tensor"),
        P("ctx", "tensor"),
        P("ctx", "tensor"),
        P("ctx", "tensor"),
        P(),
    )
    return jax.shard_map(body, mesh=mesh, in_specs=in_specs, out_specs=out_specs, check_vma=False)
```

```python
import functools
import math

import jax
import jax.numpy as jnp
import numpy as np
from jax import lax
from jax.experimental import pallas as pl
from jax.experimental.pallas import tpu as pltpu
from jax.sharding import PartitionSpec as P

HD = 128
GROUP = 128
TWO_PI = 2.0 * math.pi
LOG2E = 1.4426950408889634
SCALE = HD ** (-0.5)
MESH = pl.DeviceIdType.MESH
BF = jnp.bfloat16
F32 = jnp.float32
ANY = pl.BlockSpec(memory_space=pl.ANY)
DMA = pltpu.SemaphoreType.DMA


class Place:
    def __init__(self):
        self.ctx = lax.axis_index("ctx")
        self.dp = lax.axis_index("dp")
        self.y = lax.axis_index("tensor")
        self.x = lax.div(self.ctx, 4)
        self.zl = lax.rem(self.ctx, 4)
        self.zh = lax.div(self.dp, 2)
        self.c = lax.rem(self.dp, 2)
        self.z = self.zh * 4 + self.zl

    def xn(self, d):
        return {"ctx": lax.rem(self.x + (d + 4), 4) * 4 + self.zl, "dp": self.dp}

    def zn(self, d):
        z = lax.rem(self.z + (d + 8), 8)
        return {"ctx": self.x * 4 + lax.rem(z, 4), "dp": lax.div(z, 4) * 2 + self.c}

    def zat(self, z):
        return {"ctx": self.x * 4 + lax.rem(z, 4), "dp": lax.div(z, 4) * 2 + self.c}

    def zline(self, d):
        return {"ctx": self.x * 4 + lax.rem(self.zl + d, 4), "dp": self.dp}

    def yn(self, d):
        return {"tensor": lax.rem(self.y + (d + 4), 4)}

    def sib(self):
        return {"dp": self.zh * 2 + (1 - self.c)}

    def far(self, other):
        c = (1 - self.c) if other else self.c
        return {"dp": (1 - self.zh) * 2 + c}

    def mix(self, first, second, c):
        return {k: first[k] * (1 - c) + second[k] * c for k in first}


class Sender:
    def __init__(self, sems):
        self.sems = sems
        self.used = 0
        self.sent = []

    def make(self, index, what):
        src, dst, recv, peer = what()
        return pltpu.make_async_remote_copy(
            src_ref=src,
            dst_ref=dst,
            send_sem=self.sems.at[index],
            recv_sem=recv,
            device_id=peer,
            device_id_type=MESH,
        )

    def __call__(self, what):
        index = self.used
        self.used += 1
        self.sent.append((index, what))
        self.make(index, what).start()

    def drain(self):
        for index, what in self.sent:
            self.make(index, what).wait_send()


def arrived(ref, sem):
    pltpu.make_async_copy(ref, ref, sem).wait()


def sin_cos_turns(r):
    t = (r - jnp.floor(r + 0.5)) * TWO_PI
    q = t * t
    s = jnp.full_like(t, 1.0)
    for n in (14, 12, 10, 8, 6, 4, 2):
        s = 1.0 - q * s * (1.0 / (n * (n + 1)))
    k = jnp.full_like(t, 1.0)
    for n in (15, 13, 11, 9, 7, 5, 3, 1):
        k = 1.0 - q * k * (1.0 / (n * (n + 1)))
    return s * t, k


def spread(row):
    return jnp.broadcast_to(row, (128, row.shape[1])).T


def main_kernel(
    hid_h, pos_h, q_h, kw_h, vw_h, ks_h, vs_h, smooth_h, do_h, freq_h,
    gh_o, gq_o, gkw_o, gvw_o, gks_o, gvs_o, gsm_o,
    hid, pos, queries, kw, vw, ks, vs, smooth, dout, freq,
    cos, sin, inv, ss, st, cb,
    wbuf, sm, smt, acc, kv,
    qr, qt, do, dot_t, scr, dpr, dq, stm, stl, stu,
    a_st, a_rb, a_t, a_zs, a_z,
    hs, hr, ms, r1, r2, sx, tz, zs, zr, fb,
    y_s, y_r1, y_r2, yv, gs,
    dcol, gq, gkw, gvw, gks, gvs, gsm,
    ssem, csem, osem, nsem, sibsem, kvsem, asem, asend, azsem, hsem, r1sem, r2sem,
    zsem, fsem, y1sem, y2sem, vsem, gxsem, gzsem, gssem,
):
    p = Place()
    c = p.c
    pairs = (
        (kw_h, kw), (vw_h, vw), (ks_h, ks), (vs_h, vs), (smooth_h, smooth),
        (pos_h, pos), (freq_h, freq), (hid_h, hid), (q_h, queries), (do_h, dout),
    )
    loads = [pltpu.make_async_copy(s, d, csem.at[i]) for i, (s, d) in enumerate(pairs)]
    for load in loads:
        load.start()
    xr, xl, yr, yl, sib = p.xn(1), p.xn(-1), p.yn(1), p.yn(-1), p.sib()
    peers = [xr, xl, p.xn(2), yr, yl, p.yn(2), sib, p.far(1)]
    peers += [p.zn(k) for k in range(1, 8)]
    barrier = pltpu.get_barrier_semaphore()
    for peer in peers:
        pl.semaphore_signal(barrier, inc=1, device_id=peer, device_id_type=MESH)
    send = Sender(ssem)

    a0 = p.x * (1 - c) + p.zl * c
    b0 = p.zl * (1 - c) + p.x * c

    def slot(a, b):
        a = lax.rem(a0 + (a + 4), 4)
        b = lax.rem(b0 + (b + 4), 4)
        return (a * 4 + b) * (1 - c) + (b * 4 + a) * c

    own = slot(0, 0)
    for load in loads[:5]:
        load.wait()
    for q in range(4):
        rows = slice(q * 128, (q + 1) * 128)
        s_row = smooth[:, pl.ds(pl.multiple_of(p.ctx * 512 + q * 128, 128), 128)]
        s_col = spread(s_row)
        for half, (w_ref, step_ref) in enumerate(((kw, ks), (vw, vs))):
            cols = slice(half * HD, (half + 1) * HD)
            weight = w_ref[rows, :].astype(F32)
            step = step_ref[q : q + 1, :]
            ratio = weight * s_col / step
            sine, cosine = sin_cos_turns(ratio)
            sine = sine * (1.0 / TWO_PI)
            quant = (step * (ratio - sine)).astype(BF)
            wbuf[own * 4 + q, :, cols] = quant
            slope = 1.0 - cosine
            ss[rows, cols] = slope * s_col
            st[rows, cols] = ratio * cosine - sine
            cb[rows, cols] = slope * weight - quant.astype(F32) / s_col
    pl.semaphore_wait(barrier, len(peers))

    an = {d: p.mix(p.xn(d), p.zn(d), c) for d in (1, -1)}
    bn = {d: p.mix(p.zn(d), p.xn(d), c) for d in (1, -1)}

    def chunk(s, sub):
        return wbuf.at[s * 4 + c * 2 + sub]

    def net(s, sub, peer):
        send(lambda: (chunk(s, sub), chunk(s, sub), nsem.at[s * 2 + sub], peer))

    def got(s, sub):
        arrived(chunk(s, sub), nsem.at[s * 2 + sub])

    def to_sib(s):
        ref = wbuf.at[pl.ds(s * 4 + c * 2, 2)]
        send(lambda: (ref, ref, sibsem.at[s], sib))

    def from_sib(s):
        arrived(wbuf.at[pl.ds(s * 4 + (1 - c) * 2, 2)], sibsem.at[s])

    def dot(s, h):
        w = wbuf[pl.ds(s * 4 + h * 2, 2)].reshape(256, 256)
        acc[...] += jnp.dot(sm[s * 2 + h], w, preferred_element_type=F32)

    for sub in (0, 1):
        net(own, sub, an[1])
        net(own, 1 - sub, an[-1])
        net(own, sub, bn[1])
        net(own, 1 - sub, bn[-1])

    def prepare(j0, j1):
        for j in range(j0, j1):
            cols = slice(j * 256, (j + 1) * 256)
            block = hid[:, cols].astype(F32) * inv[:, cols]
            sm[j] = block.astype(BF)
            smt[j] = block.T.astype(BF)

    inv[...] = 1.0 / smooth[...]
    for load in loads[5:7]:
        load.wait()
    angle = spread(pos[...].astype(F32)) * freq[...]
    cos[...] = jnp.cos(angle)
    turned = jnp.sin(angle)
    lane = lax.broadcasted_iota(jnp.int32, (128, 128), 1)
    sin[...] = jnp.where(lane < HD // 2, -turned, turned)

    left, right, far = slot(-1, 0), slot(1, 0), slot(2, 0)
    got(left, 0)
    net(left, 0, an[1])
    got(right, 1)
    net(right, 1, an[-1])
    for s, sub in ((left, 0), (right, 1)):
        net(s, sub, bn[1])
        net(s, sub, bn[-1])
    loads[7].wait()
    prepare(0, 8)
    for s, sub in ((left, 1), (right, 0)):
        got(s, sub)
        net(s, sub, bn[1])
        net(s, sub, bn[-1])
        to_sib(s)

    def across(a):
        bl, br = slot(a, -1), slot(a, 1)
        got(bl, 0)
        net(bl, 0, bn[1])
        got(br, 1)
        net(br, 1, bn[-1])
        got(bl, 1)
        got(br, 0)
        to_sib(bl)
        to_sib(br)
        return bl, br

    ready = [*across(0), left, right]
    for sub in (0, 1):
        got(far, sub)
        net(far, sub, bn[1])
        net(far, sub, bn[-1])
    to_sib(far)
    ready.append(far)
    prepare(8, 20)
    ready += across(-1)
    prepare(20, 32)
    acc[...] = jnp.zeros_like(acc)
    dot(own, 0)
    dot(own, 1)
    ready += across(1)
    for s in ready[:5]:
        dot(s, c)
    ready += across(2)
    for s in ready[5:]:
        dot(s, c)
    for a in (0, -1, 1, 2):
        s = slot(a, 2)
        got(s, 0)
        got(s, 1)
        to_sib(s)
        dot(s, c)
    for a in (-1, 1, 0, 2):
        for b in (0, -1, 1, 2):
            if a == 0 and b == 0:
                continue
            s = slot(b, a)
            from_sib(s)
            dot(s, 1 - c)

    key_raw = acc[:, :HD]
    rotated = key_raw * cos[...] + pltpu.roll(key_raw, HD // 2, 1) * sin[...]
    kv[p.ctx, :, :HD] = rotated.astype(BF)
    kv[p.ctx, :, HD:] = acc[:, HD:].astype(BF)

    def kslot(d, k):
        return lax.rem(p.x + (d + 4), 4) * 4 + lax.rem(p.zl + k, 4)

    def ksend(d, k, peer):
        def what():
            s = kslot(d, k)
            return kv.at[s], kv.at[s], kvsem.at[s], peer()

        send(what)

    def kgot(d, k):
        s = kslot(d, k)
        arrived(kv.at[s], kvsem.at[s])

    to_right, to_left = (lambda: p.xn(1)), (lambda: p.xn(-1))
    ksend(0, 0, to_right)
    ksend(0, 0, to_left)
    for k in (2, 1, 3):
        ksend(0, 0, functools.partial(p.zline, k))

    groups = qr.shape[0] // 128
    for load in loads[8:]:
        load.wait()
    for g in range(groups):
        cols = slice(g * 128, (g + 1) * 128)
        q = queries[:, cols].astype(F32)
        q = q * cos[...] + pltpu.roll(q, HD // 2, 1) * sin[...]
        qr[cols, :] = q.astype(BF)
        qt[:, cols] = q.T.astype(BF)
        d = dout[:, cols]
        do[cols, :] = d
        dot_t[:, cols] = d.astype(F32).T.astype(BF)
    width = 256
    chunks = qr.shape[0] // width
    q_index = p.ctx * 128 + lax.rem(lax.broadcasted_iota(jnp.int32, (1, width), 1), 128)
    first = q_index - jnp.concatenate([pos[...]] * (width // 128), axis=1)
    row = lax.broadcasted_iota(jnp.int32, (256, width), 0)
    stm[...] = jnp.full_like(stm, -1e30)
    stl[...] = jnp.zeros_like(stl)
    stu[...] = jnp.zeros_like(stu)

    def stats(j):
        kj = kv[pl.ds(j * 2, 2), :, :HD].reshape(256, HD)
        vj = kv[pl.ds(j * 2, 2), :, HD:].reshape(256, HD)
        k_index = row + j * 256
        allowed = (k_index <= q_index) & (k_index >= first)
        for n in range(chunks):
            cols = slice(n * width, (n + 1) * width)
            m = stm[:, cols]
            s = jnp.dot(kj, qt[:, cols], preferred_element_type=F32) * (SCALE * LOG2E)
            s = jnp.where(allowed, s, -1e30)
            d = jnp.dot(vj, dot_t[:, cols], preferred_element_type=F32)
            scr[j, :, cols] = s
            dpr[j, :, cols] = d
            m_new = jnp.maximum(m, jnp.max(s, axis=0, keepdims=True))
            e = jnp.where(allowed, jnp.exp2(s - m_new), 0.0)
            fix = jnp.exp2(m - m_new)
            stm[:, cols] = m_new
            stl[:, cols] = stl[:, cols] * fix + jnp.sum(e, axis=0, keepdims=True)
            stu[:, cols] = stu[:, cols] * fix + jnp.sum(e * d, axis=0, keepdims=True)

    def group_step(g, _):
        @pl.when(g == 0)
        def _():
            for k in (1, 3, 2):
                kgot(0, k)
                ksend(0, k, to_right)
                ksend(0, k, to_left)

        @pl.when(g == 1)
        def _():
            for k in (0, 1, 3, 2):
                kgot(-1, k)
                if k in (0, 2):
                    ksend(-1, k, to_right)
                kgot(1, k)
                if k in (1, 3):
                    ksend(1, k, to_left)

        @pl.when(g == 3)
        def _():
            for k in (0, 1, 3, 2):
                kgot(2, k)

        d = g + lax.div(g, 2) - 2 * lax.div(g, 3)

        def pair_step(r, _):
            j = lax.rem(p.x + d, 4) * 2 + r

            @pl.when(j * 2 <= p.ctx)
            def _():
                stats(j)

            return 0

        return lax.fori_loop(0, 2, pair_step, 0)

    lax.fori_loop(0, 4, group_step, 0)

    shift = [stm[:, n * width : (n + 1) * width] for n in range(chunks)]
    delta = []
    for n in range(chunks):
        cols = slice(n * width, (n + 1) * width)
        shift[n] = shift[n] + jnp.log2(stl[:, cols])
        delta.append(stu[:, cols] / stl[:, cols])
    for n in range(chunks):
        cols = slice(n * width, (n + 1) * width)
        stm[:, cols] = shift[n]
        stu[:, cols] = delta[n]
    dq[...] = jnp.zeros_like(dq)

    def acopy(t):
        peer = p.mix(p.xn(1), p.xn(-1), lax.rem(t, 2))
        return pltpu.make_async_remote_copy(
            src_ref=a_st.at[t],
            dst_ref=a_rb.at[t],
            send_sem=asend.at[t],
            recv_sem=asem.at[t],
            device_id=peer,
            device_id_type=MESH,
        )

    def grads(t, _):
        q, r = lax.div(t, 2), lax.rem(t, 2)
        middle = lax.div(q * (3 - q), 2)
        d = middle * (1 + 2 * r) + (1 - middle) * lax.div((3 - q) * 2, 3)
        flip = middle * (2 - q)
        h = r + flip * (1 - 2 * r)
        j = lax.rem(p.x + d, 4) * 2 + h

        @pl.when(j * 2 <= p.ctx)
        def _():
            kj = kv[pl.ds(j * 2, 2), :, :HD].reshape(256, HD)
            kt = kj.astype(F32).T.astype(BF)
            dk = jnp.zeros((256, HD), F32)
            dv = jnp.zeros((256, HD), F32)
            for n in range(chunks):
                cols = slice(n * width, (n + 1) * width)
                prob = jnp.exp2(scr[j, :, cols] - stm[:, cols])
                ds = (prob * (dpr[j, :, cols] - stu[:, cols])).astype(BF)
                dv += jnp.dot(prob.astype(BF), do[cols, :], preferred_element_type=F32)
                dk += jnp.dot(ds, qr[cols, :], preferred_element_type=F32)
                dq[:, cols] += jnp.dot(kt, ds, preferred_element_type=F32)
            a_st[t, :, :, :HD] = (dk * SCALE).astype(BF).reshape(2, 128, HD)
            a_st[t, :, :, HD:] = dv.astype(BF).reshape(2, 128, HD)

        @pl.when(j * 2 > p.ctx)
        def _():
            a_st[t] = jnp.zeros((2, 128, 2 * HD), BF)

        @pl.when(q == 2)
        def _():
            arrived(a_rb.at[t - 4], asem.at[t - 4])
            a_st[t] = (a_st[t].astype(F32) + a_rb[t - 4].astype(F32)).astype(BF)

        @pl.when(t < 6)
        def _():
            acopy(t).start()

        return 0

    lax.fori_loop(0, 8, grads, 0)

    for g in range(groups):
        cols = slice(g * 128, (g + 1) * 128)
        t = dq[:, cols].T * SCALE
        gq[:, cols] = t * cos[...] - pltpu.roll(t, HD // 2, 1) * sin[...]
    stores = [pltpu.make_async_copy(gq, gq_o, osem.at[0])]
    stores[0].start()

    for t in (2, 3, 4, 5):
        arrived(a_rb.at[t], asem.at[t])
    for h, (near, run) in enumerate(((3, 4), (2, 5))):
        total = a_st[6 + h].astype(F32) + a_rb[near].astype(F32) + a_rb[run].astype(F32)
        a_t[h * 2 : h * 2 + 2] = total
        a_zs[h * 2 : h * 2 + 2] = total.astype(BF)
    for k in (2, 1, 3):
        send(
            functools.partial(
                lambda k: (
                    a_zs.at[lax.rem(p.zl + k, 4)], a_z.at[k - 1], azsem.at[k - 1], p.zline(k)
                ),
                k,
            )
        )
    d_kv = a_t[p.zl]
    for k in (1, 3, 2):
        arrived(a_z.at[k - 1], azsem.at[k - 1])
        d_kv += a_z[k - 1].astype(F32)
    dk = d_kv[:, :HD]
    dk = dk * cos[...] - pltpu.roll(dk, HD // 2, 1) * sin[...]
    g = jnp.concatenate([dk, d_kv[:, HD:]], axis=1).astype(BF)

    dirs = (2, 1, -1, 0)

    def wgrad(k):
        blk = lax.rem(p.x + (dirs[k] + 4), 4)
        for zl in range(4):
            j = (blk * 4 + zl) * 2
            his = jnp.dot(smt[j + (1 - c)], g, preferred_element_type=F32).astype(BF)
            mine = jnp.dot(smt[j + c], g, preferred_element_type=F32).astype(BF)
            for u in (0, 1):
                hs[u, k, zl] = his[u * 128 : u * 128 + 128]
                ms[u, k, zl] = mine[u * 128 : u * 128 + 128]

    def hsend(u, k):
        send(lambda: (hs.at[u, k], hr.at[u, k], hsem.at[u, k], sib))

    def hgot(u, k):
        arrived(hr.at[u, k], hsem.at[u, k])

    def both(u, k, h):
        part = slice(h * 2, h * 2 + 2)
        return ms[u, k, part].astype(F32) + hr[u, k, part].astype(F32)

    def xstage(u, k, h, extra=None):
        value = both(u, k, h)
        if extra is not None:
            value = value + extra.astype(F32)
        sx[u, k, h] = value.astype(BF)

    def xfirst(u):
        hgot(u, 0)
        for h in (0, 1):
            xstage(u, 0, h)
            peer = (xr, xl)[h]
            send(
                functools.partial(
                    lambda h, peer: (sx.at[u, 0, h], r1.at[u, h], r1sem.at[u, h], peer), h, peer
                )
            )

    def xraw(u):
        hgot(u, 1)
        xstage(u, 1, 1)
        send(lambda: (sx.at[u, 1, 1], r2.at[u, 0, 1], r2sem.at[u, 1], xr))
        hgot(u, 2)
        xstage(u, 2, 0)
        send(lambda: (sx.at[u, 2, 0], r2.at[u, 1, 0], r2sem.at[u, 2], xl))

    def xrun(u):
        arrived(r1.at[u, 0], r1sem.at[u, 0])
        xstage(u, 1, 0, r1[u, 0])
        send(lambda: (sx.at[u, 1, 0], r2.at[u, 0, 0], r2sem.at[u, 0], xr))
        arrived(r1.at[u, 1], r1sem.at[u, 1])
        xstage(u, 2, 1, r1[u, 1])
        send(lambda: (sx.at[u, 2, 1], r2.at[u, 1, 1], r2sem.at[u, 3], xl))

    def zsend(u):
        hgot(u, 3)
        for i, (s, h) in ((1, (0, 1)), (2, (1, 0)), (0, (0, 0)), (3, (1, 1))):
            arrived(r2.at[u, s, h], r2sem.at[u, i])
        for h in (0, 1):
            total = both(u, 3, h) + r2[u, 0, h].astype(F32) + r2[u, 1, h].astype(F32)
            tz[u, h * 2 : h * 2 + 2] = total
            zs[u, h * 2 : h * 2 + 2] = total.astype(BF)

        def what(k):
            zl = lax.rem(p.zl + k, 4)
            return zs.at[u, zl], zr.at[p.z], zsem.at[p.z], p.zat(u * 4 + zl)

        for k in (2, 1, 3):
            send(functools.partial(what, k))

        @pl.when(p.zh != u)
        def _():
            Sender.make(send, 60 + u, lambda: what(0)).start()

    def dgrad(d, h):
        blk = lax.rem(p.y + (d + 4), 4) * 16 + h * 8
        out = []
        for i in range(4):
            wb = wbuf[pl.ds(blk + i * 2, 2)].reshape(256, 256)
            out.append(
                lax.dot_general(g, wb, (((1,), (1,)), ((), ())), preferred_element_type=F32)
            )
        return out

    def dstore(k, d, h, extra=None):
        for i, piece in enumerate(dgrad(d, h)):
            cols = slice(i * 256, (i + 1) * 256)
            if extra is not None:
                piece = piece + extra[:, cols].astype(F32)
            y_s[k, h, :, cols] = piece.astype(BF)

    for k in range(4):
        wgrad(k)
        hsend(0, k)
    for k in range(4):
        hsend(1, k)
    xfirst(0)
    xraw(0)
    dstore(0, 2, 0)
    send(lambda: (y_s.at[0, 0], y_r1.at[0], y1sem.at[0], yr))
    xrun(0)
    xfirst(1)
    xraw(1)
    dstore(0, 2, 1)
    send(lambda: (y_s.at[0, 1], y_r1.at[1], y1sem.at[1], yl))
    dstore(1, 1, 1)
    send(lambda: (y_s.at[1, 1], y_r2.at[0, 1], y2sem.at[1], yr))
    dstore(2, -1, 0)
    send(lambda: (y_s.at[2, 0], y_r2.at[1, 0], y2sem.at[2], yl))
    xrun(1)
    arrived(y_r1.at[0], y1sem.at[0])
    dstore(1, 1, 0, y_r1.at[0])
    send(lambda: (y_s.at[1, 0], y_r2.at[0, 0], y2sem.at[0], yr))
    zsend(0)
    arrived(y_r1.at[1], y1sem.at[1])
    dstore(2, -1, 1, y_r1.at[1])
    send(lambda: (y_s.at[2, 1], y_r2.at[1, 1], y2sem.at[3], yl))
    for h in (0, 1):
        for i, piece in enumerate(dgrad(0, h)):
            dcol[:, h * 1024 + i * 256 : h * 1024 + (i + 1) * 256] = piece
    zsend(1)

    mine = c * 2 + p.zh
    f = tz[p.zh, p.zl]
    for k in (1, 7, 2, 6, 3, 5, 4):
        z = lax.rem(p.z + k, 8)
        arrived(zr.at[z], zsem.at[z])
        f += zr[z].astype(F32)
    fb[mine] = f.astype(BF)
    for i, peer in ((0, p.far(0)), (1, p.far(1)), (2, sib)):
        send(
            functools.partial(lambda i, peer: (fb.at[mine], fb.at[mine], fsem.at[i], peer), i, peer)
        )

    t = f * cb[pl.ds(pl.multiple_of(mine * 128, 128), 128), :]
    t = t[:, :HD] + t[:, HD:]
    yv[p.y] = jnp.broadcast_to(jnp.sum(t.T, axis=0, keepdims=True), (8, 128))
    for k in (2, 1, 3):
        send(functools.partial(lambda k: (yv.at[p.y], yv.at[p.y], vsem.at[k - 1], p.yn(k)), k))

    for i, (s, h) in ((1, (0, 1)), (2, (1, 0)), (0, (0, 0)), (3, (1, 1))):
        arrived(y_r2.at[s, h], y2sem.at[i])
    inv_cols = inv[:, pl.ds(pl.multiple_of(p.y * 2048, 2048), 2048)]
    for h in (0, 1):
        cols = slice(h * 1024, (h + 1) * 1024)
        total = dcol[:, cols] + y_r2[0, h].astype(F32) + y_r2[1, h].astype(F32)
        dcol[:, cols] = total * inv_cols[:, cols]
    stores.append(pltpu.make_async_copy(dcol, gh_o, osem.at[1]))
    stores[-1].start()

    for k in (1, 3, 2):
        arrived(yv.at[lax.rem(p.y + (4 - k), 4)], vsem.at[k - 1])
    gs[c, p.z, p.x] = (yv[0] + yv[1]) + (yv[2] + yv[3])
    for k in (2, 1, 3):
        send(
            functools.partial(
                lambda k: (
                    gs.at[c, p.z, p.x], gs.at[c, p.z, p.x], gxsem.at[k - 1], p.xn(k)
                ),
                k,
            )
        )
    for k in (1, 3, 2):
        arrived(gs.at[c, p.z, lax.rem(p.x + (4 - k), 4)], gxsem.at[k - 1])
    for k in (4, 3, 5, 2, 6, 1, 7):
        send(
            functools.partial(
                lambda k: (gs.at[c, p.z], gs.at[c, p.z], gzsem.at[k - 1], p.zn(k)), k
            )
        )

    arrived(fb.at[(1 - c) * 2 + p.zh], fsem.at[2])
    arrived(fb.at[c * 2 + (1 - p.zh)], fsem.at[0])
    arrived(fb.at[(1 - c) * 2 + (1 - p.zh)], fsem.at[1])
    for q in range(4):
        rows = slice(q * 128, (q + 1) * 128)
        f = fb[q].astype(F32)
        o = f * ss[rows, :]
        gkw[rows, :] = o[:, :HD]
        gvw[rows, :] = o[:, HD:]
        o = jnp.sum(f * st[rows, :], axis=0, keepdims=True)
        gks[q : q + 1, :] = o[:, :HD]
        gvs[q : q + 1, :] = o[:, HD:]
    for i, (src, dst) in enumerate(((gkw, gkw_o), (gvw, gvw_o), (gks, gks_o), (gvs, gvs_o))):
        stores.append(pltpu.make_async_copy(src, dst, osem.at[2 + i]))
        stores[-1].start()

    for k in (1, 7, 2, 6, 3, 5, 4):
        arrived(gs.at[c, lax.rem(p.z + (8 - k), 8)], gzsem.at[k - 1])
    send(lambda: (gs.at[c], gs.at[c], gssem.at[0], sib))
    arrived(gs.at[1 - c], gssem.at[0])
    for i in range(16):
        for q in range(4):
            r = i * 4 + q
            gsm[r : r + 1, :] = gs[q // 2, (q % 2) * 4 + i % 4, i // 4, :1, :]
    stores.append(pltpu.make_async_copy(gsm, gsm_o, osem.at[6]))
    stores[-1].start()

    send.drain()
    for u in (0, 1):

        @pl.when(p.zh != u)
        def _():
            send.make(
                60 + u, lambda: (zs.at[u, p.zl], zr.at[p.z], zsem.at[p.z], p.zat(u * 4 + p.zl))
            ).wait_send()

    for t in range(6):
        acopy(t).wait_send()
    for store in stores:
        store.wait()


def main_call(*args):
    rows = args[2].shape[1]
    outs = (
        ((128, 2048), F32), ((128, rows), F32), ((512, 128), F32), ((512, 128), F32),
        ((4, 128), F32), ((4, 128), F32), ((64, 128), F32),
    )
    scratch = [pltpu.VMEM(a.shape, a.dtype) for a in args]
    scratch += [pltpu.VMEM(*s) for s in (
        ((128, 128), F32), ((128, 128), F32), ((1, 8192), F32),
        ((512, 256), F32), ((512, 256), F32), ((512, 256), F32),
        ((64, 128, 256), BF), ((32, 128, 256), BF), ((32, 256, 128), BF), ((128, 256), F32),
        ((16, 128, 256), BF),
        ((rows, HD), BF), ((HD, rows), BF), ((rows, HD), BF), ((HD, rows), BF),
        ((8, 256, rows), F32), ((8, 256, rows), F32), ((HD, rows), F32),
        ((1, rows), F32), ((1, rows), F32), ((1, rows), F32),
        ((8, 2, 128, 256), BF), ((6, 2, 128, 256), BF), ((4, 128, 256), F32),
        ((4, 128, 256), BF), ((3, 128, 256), BF),
        ((2, 4, 4, 128, 256), BF), ((2, 4, 4, 128, 256), BF), ((2, 4, 4, 128, 256), BF),
        ((2, 2, 2, 128, 256), BF), ((2, 2, 2, 2, 128, 256), BF), ((2, 3, 2, 2, 128, 256), BF),
        ((2, 4, 128, 256), F32), ((2, 4, 128, 256), BF), ((8, 128, 256), BF),
        ((4, 128, 256), BF),
        ((3, 2, 128, 1024), BF), ((2, 128, 1024), BF), ((2, 2, 128, 1024), BF),
        ((4, 8, 128), F32), ((2, 8, 4, 8, 128), F32),
    )]
    scratch += [pltpu.VMEM(*o) for o in outs]
    scratch += [DMA(s) for s in (
        (128,), (10,), (7,), (32,), (16,), (16,), (6,), (6,), (3,), (2, 4), (2, 2), (2, 4),
        (8,), (3,), (2,), (4,), (3,), (3,), (7,), (1,),
    )]
    return pl.pallas_call(
        main_kernel,
        name="main",
        out_shape=tuple(jax.ShapeDtypeStruct(*o) for o in outs),
        in_specs=[ANY] * len(args),
        out_specs=(ANY,) * len(outs),
        scratch_shapes=scratch,
        compiler_params=pltpu.CompilerParams(
            collective_id=0, has_side_effects=True, vmem_limit_bytes=60 << 20
        ),
    )(*args)


def finish_kernel(*refs):
    count = (len(refs) - 1) // 3
    sems = refs[-1]
    loads, stores = [], []
    for i in range(count):
        held = refs[2 * count + i]
        loads.append(pltpu.make_async_copy(refs[i], held, sems.at[0, i]))
        stores.append(pltpu.make_async_copy(held, refs[count + i], sems.at[1, i]))
    for load in loads:
        load.start()
    for load, store in zip(loads, stores):
        load.wait()
        store.start()
    for store in stores:
        store.wait()


def finish(*arrays):
    return pl.pallas_call(
        finish_kernel,
        name="finish",
        out_shape=tuple(jax.ShapeDtypeStruct(a.shape, a.dtype) for a in arrays),
        in_specs=[ANY] * len(arrays),
        out_specs=(ANY,) * len(arrays),
        scratch_shapes=[pltpu.VMEM(a.shape, a.dtype) for a in arrays] + [DMA((2, len(arrays)))],
        compiler_params=pltpu.CompilerParams(vmem_limit_bytes=60 << 20),
    )(*arrays)


def body(
    hidden_states,
    positions,
    queries,
    key_weight,
    value_weight,
    key_step,
    value_step,
    smoothing,
    grad_out,
):
    index = np.arange(HD) % (HD // 2)
    freq = jnp.asarray((10000.0 ** (-2.0 * index / HD)).astype(np.float32))[None, :]
    gh, gq, gkw, gvw, gks, gvs, gsm = finish(
        *main_call(
            hidden_states[0], positions, queries[0], key_weight, value_weight, key_step,
            value_step, smoothing[None, :], grad_out[0], freq,
        )
    )
    return gh[None], gq[None], gkw, gvw, gks, gvs, gsm.reshape(smoothing.shape)


def solution(mesh):
    in_specs = (
        P("dp", "ctx", None),
        P("dp", "ctx"),
        P("dp", "ctx", "tensor"),
        P("ctx", "tensor"),
        P("ctx", "tensor"),
        P("ctx", "tensor"),
        P("ctx", "tensor"),
        P(),
        P("dp", "ctx", "tensor"),
    )
    out_specs = (
        P("dp", "ctx", "tensor"),
        P("dp", "ctx", "tensor"),
        P("ctx", "tensor"),
        P("ctx", "tensor"),
        P("ctx", "tensor"),
        P("ctx", "tensor"),
        P(),
    )
    return jax.shard_map(body, mesh=mesh, in_specs=in_specs, out_specs=out_specs, check_vma=False)
```

```python
import functools
import math

import jax
import jax.numpy as jnp
import numpy as np
from jax import lax
from jax.experimental import pallas as pl
from jax.experimental.pallas import tpu as pltpu
from jax.sharding import PartitionSpec as P

HD = 128
GROUP = 128
TWO_PI = 2.0 * math.pi
LOG2E = 1.4426950408889634
SCALE = HD ** (-0.5)
MESH = pl.DeviceIdType.MESH
BF = jnp.bfloat16
F32 = jnp.float32
ANY = pl.BlockSpec(memory_space=pl.ANY)
DMA = pltpu.SemaphoreType.DMA


class Place:
    def __init__(self):
        self.ctx = lax.axis_index("ctx")
        self.dp = lax.axis_index("dp")
        self.y = lax.axis_index("tensor")
        self.x = lax.div(self.ctx, 4)
        self.zl = lax.rem(self.ctx, 4)
        self.zh = lax.div(self.dp, 2)
        self.c = lax.rem(self.dp, 2)
        self.z = self.zh * 4 + self.zl

    def xn(self, d):
        return {"ctx": lax.rem(self.x + (d + 4), 4) * 4 + self.zl, "dp": self.dp}

    def zn(self, d):
        z = lax.rem(self.z + (d + 8), 8)
        return {"ctx": self.x * 4 + lax.rem(z, 4), "dp": lax.div(z, 4) * 2 + self.c}

    def at(self, dx, k):
        return {
            "ctx": lax.rem(self.x + (dx + 4), 4) * 4 + lax.rem(self.zl + k, 4), "dp": self.dp
        }

    def zline(self, d):
        return {"ctx": self.x * 4 + lax.rem(self.zl + d, 4), "dp": self.dp}

    def yn(self, d):
        return {"tensor": lax.rem(self.y + (d + 4), 4)}

    def sib(self):
        return {"dp": self.zh * 2 + (1 - self.c)}

    def far(self, other):
        c = (1 - self.c) if other else self.c
        return {"dp": (1 - self.zh) * 2 + c}

    def mix(self, first, second, c):
        return {k: first[k] * (1 - c) + second[k] * c for k in first}


class Sender:
    def __init__(self, sems):
        self.sems = sems
        self.used = 0
        self.sent = []

    def make(self, index, what):
        src, dst, recv, peer = what()
        return pltpu.make_async_remote_copy(
            src_ref=src,
            dst_ref=dst,
            send_sem=self.sems.at[index],
            recv_sem=recv,
            device_id=peer,
            device_id_type=MESH,
        )

    def __call__(self, what):
        index = self.used
        self.used += 1
        self.sent.append((index, what))
        self.make(index, what).start()

    def drain(self):
        for index, what in self.sent:
            self.make(index, what).wait_send()


def arrived(ref, sem):
    pltpu.make_async_copy(ref, ref, sem).wait()


def sin_cos_turns(r):
    t = (r - jnp.floor(r + 0.5)) * TWO_PI
    q = t * t
    s = jnp.full_like(t, 1.0)
    for n in (14, 12, 10, 8, 6, 4, 2):
        s = 1.0 - q * s * (1.0 / (n * (n + 1)))
    k = jnp.full_like(t, 1.0)
    for n in (15, 13, 11, 9, 7, 5, 3, 1):
        k = 1.0 - q * k * (1.0 / (n * (n + 1)))
    return s * t, k


def spread(row):
    return jnp.broadcast_to(row, (128, row.shape[1])).T


def main_kernel(
    hid_h, pos_h, q_h, kw_h, vw_h, ks_h, vs_h, smooth_h, do_h, freq_h,
    gh_o, gq_o, gkw_o, gvw_o, gks_o, gvs_o, gsm_o,
    hid, pos, queries, kw, vw, ks, vs, smooth, dout, freq,
    cos, sin, inv, ss, st, cb,
    wbuf, sm, smt, smf, acc, kv, gall,
    qr, qt, do, dot_t, scr, dpr, dq, stm, stl, stu,
    a_st, a_rb, a_t, a_zs, a_z,
    wg, hs, hr, fs, fr, fb,
    y_s, y_r1, y_r2, yv, vp, gs,
    dcol, gq, gkw, gvw, gks, gvs, gsm,
    ssem, csem, osem, nsem, sibsem, kvsem, gsem, tsem, tysem, asem, asend, azsem,
    fsem, y1sem, y2sem, vsem, vpsem, gxsem, gzsem,
):
    p = Place()
    c = p.c
    pairs = (
        (kw_h, kw), (vw_h, vw), (ks_h, ks), (vs_h, vs), (smooth_h, smooth),
        (pos_h, pos), (freq_h, freq), (hid_h, hid), (q_h, queries), (do_h, dout),
    )
    loads = [pltpu.make_async_copy(s, d, csem.at[i]) for i, (s, d) in enumerate(pairs)]
    for load in loads:
        load.start()
    xr, xl, yr, yl, sib = p.xn(1), p.xn(-1), p.yn(1), p.yn(-1), p.sib()
    peers = [yr, yl, p.yn(2), sib, p.zn(1), p.zn(-1), p.zn(2), p.zn(-2), p.far(0)]
    peers += [p.at(dx, k) for dx in range(4) for k in range(4) if dx or k]
    barrier = pltpu.get_barrier_semaphore()
    for peer in peers:
        pl.semaphore_signal(barrier, inc=1, device_id=peer, device_id_type=MESH)
    send = Sender(ssem)

    a0 = p.x * (1 - c) + p.zl * c
    b0 = p.zl * (1 - c) + p.x * c

    def slot(a, b):
        a = lax.rem(a0 + (a + 4), 4)
        b = lax.rem(b0 + (b + 4), 4)
        return (a * 4 + b) * (1 - c) + (b * 4 + a) * c

    own = slot(0, 0)
    for load in loads[:5]:
        load.wait()

    def quantize(q):
        rows = pl.ds(pl.multiple_of(q * 128, 128), 128)
        s_row = smooth[:, pl.ds(pl.multiple_of(p.ctx * 512 + q * 128, 128), 128)]
        s_col = spread(s_row)
        for half, (w_ref, step_ref) in enumerate(((kw, ks), (vw, vs))):
            cols = slice(half * HD, (half + 1) * HD)
            weight = w_ref[rows, :].astype(F32)
            step = step_ref[pl.ds(q, 1), :]
            ratio = weight * s_col / step
            sine, cosine = sin_cos_turns(ratio)
            sine = sine * (1.0 / TWO_PI)
            quant = (step * (ratio - sine)).astype(BF)
            wbuf[own * 4 + q, :, cols] = quant
            slope = 1.0 - cosine
            ss[rows, cols] = slope * s_col
            st[rows, cols] = ratio * cosine - sine
            cb[rows, cols] = slope * weight - quant.astype(F32) / s_col

    quantize(c * 2)
    quantize(c * 2 + 1)
    pl.semaphore_wait(barrier, len(peers))

    an = {d: p.mix(p.xn(d), p.zn(d), c) for d in (1, -1)}
    bn = {d: p.mix(p.zn(d), p.xn(d), c) for d in (1, -1)}

    def chunk(s, sub):
        return wbuf.at[s * 4 + c * 2 + sub]

    def net(s, sub, peer):
        send(lambda: (chunk(s, sub), chunk(s, sub), nsem.at[s * 2 + sub], peer))

    def got(s, sub):
        arrived(chunk(s, sub), nsem.at[s * 2 + sub])

    def to_sib(s):
        ref = wbuf.at[pl.ds(s * 4 + c * 2, 2)]
        send(lambda: (ref, ref, sibsem.at[s], sib))

    def from_sib(s):
        arrived(wbuf.at[pl.ds(s * 4 + (1 - c) * 2, 2)], sibsem.at[s])

    def dot(s, h):
        w = wbuf[pl.ds(s * 4 + h * 2, 2)].reshape(256, 256)
        acc[...] += jnp.dot(sm[s * 2 + h], w, preferred_element_type=F32)

    for sub in (0, 1):
        net(own, sub, an[1])
        net(own, 1 - sub, an[-1])
        net(own, sub, bn[1])
        net(own, 1 - sub, bn[-1])

    def prepare(j0, j1):
        for j in range(j0, j1):
            cols = slice(j * 256, (j + 1) * 256)
            block = hid[:, cols].astype(F32) * inv[:, cols]
            sm[j] = block.astype(BF)

    inv[...] = 1.0 / smooth[...]
    left, right, far = slot(-1, 0), slot(1, 0), slot(2, 0)
    got(left, 0)
    net(left, 0, an[1])
    got(right, 1)
    net(right, 1, an[-1])
    for s, sub in ((left, 0), (right, 1)):
        net(s, sub, bn[1])
        net(s, sub, bn[-1])
    quantize((1 - c) * 2)
    quantize((1 - c) * 2 + 1)
    for s, sub in ((left, 1), (right, 0)):
        got(s, sub)
        net(s, sub, bn[1])
        net(s, sub, bn[-1])
        to_sib(s)
    loads[7].wait()
    prepare(0, 6)

    def across(a):
        bl, br = slot(a, -1), slot(a, 1)
        got(bl, 0)
        net(bl, 0, bn[1])
        got(br, 1)
        net(br, 1, bn[-1])
        got(bl, 1)
        got(br, 0)
        to_sib(bl)
        to_sib(br)
        return bl, br

    ready = [*across(0), left, right]
    for sub in (0, 1):
        got(far, sub)
        net(far, sub, bn[1])
        net(far, sub, bn[-1])
    to_sib(far)
    ready.append(far)
    prepare(6, 24)
    for load in loads[5:7]:
        load.wait()
    angle = spread(pos[...].astype(F32)) * freq[...]
    cos[...] = jnp.cos(angle)
    turned = jnp.sin(angle)
    lane = lax.broadcasted_iota(jnp.int32, (128, 128), 1)
    sin[...] = jnp.where(lane < HD // 2, -turned, turned)

    ready += across(-1)
    prepare(24, 32)
    groups = qr.shape[0] // 128
    for load in loads[8:]:
        load.wait()
    for g in range(groups):
        cols = slice(g * 128, (g + 1) * 128)
        q = queries[:, cols].astype(F32)
        q = q * cos[...] + pltpu.roll(q, HD // 2, 1) * sin[...]
        qr[cols, :] = q.astype(BF)
        qt[:, cols] = q.T.astype(BF)
        d = dout[:, cols]
        do[cols, :] = d
        dot_t[:, cols] = d.astype(F32).T.astype(BF)
    acc[...] = jnp.zeros_like(acc)
    dot(own, 0)
    dot(own, 1)
    ready += across(1)

    for s in ready[:5]:
        dot(s, c)
    ready += across(2)
    for s in ready[5:]:
        dot(s, c)
    for a in (-1, 1, 0, 2):
        for b in (0, -1, 1):
            if a == 0 and b == 0:
                continue
            s = slot(b, a)
            from_sib(s)
            dot(s, 1 - c)
    for a in (0, -1, 1, 2):
        s = slot(a, 2)
        got(s, 0)
        got(s, 1)
        to_sib(s)
        dot(s, c)
    for a in (-1, 1, 0, 2):
        s = slot(2, a)
        from_sib(s)
        dot(s, 1 - c)

    key_raw = acc[:, :HD]
    rotated = key_raw * cos[...] + pltpu.roll(key_raw, HD // 2, 1) * sin[...]
    kv[p.ctx, :, :HD] = rotated.astype(BF)
    kv[p.ctx, :, HD:] = acc[:, HD:].astype(BF)

    def kslot(d, k):
        return lax.rem(p.x + (d + 4), 4) * 4 + lax.rem(p.zl + k, 4)

    def ksend(d, k, peer, buf=kv, sem=kvsem):
        def what():
            s = kslot(d, k)
            return buf.at[s], buf.at[s], sem.at[s], peer()

        send(what)

    def kgot(d, k, buf=kv, sem=kvsem):
        s = kslot(d, k)
        arrived(buf.at[s], sem.at[s])

    to_right, to_left = (lambda: p.xn(1)), (lambda: p.xn(-1))
    ksend(0, 0, to_right)
    ksend(0, 0, to_left)
    for k in (2, 1, 3):
        ksend(0, 0, functools.partial(p.zline, k))

    for j in range(32):
        smt[j * 2 : j * 2 + 2] = sm[j].astype(F32).T.astype(BF).reshape(2, 128, 128)
    smf[p.y, :, pl.ds(pl.multiple_of(p.ctx * 128, 128), 128)] = smt[p.ctx * 4 + p.y]
    width = 256
    chunks = qr.shape[0] // width
    q_index = p.ctx * 128 + lax.rem(lax.broadcasted_iota(jnp.int32, (1, width), 1), 128)
    first = q_index - jnp.concatenate([pos[...]] * (width // 128), axis=1)
    row = lax.broadcasted_iota(jnp.int32, (256, width), 0)
    def token_send(dx, k):
        def what():
            dest = lax.rem(p.x + dx, 4) * 4 + lax.rem(p.zl + k, 4)
            cols = pl.ds(pl.multiple_of(p.ctx * 128, 128), 128)
            return smt.at[dest * 4 + p.y], smf.at[p.y, :, cols], tsem.at[p.ctx], p.at(dx, k)

        send(what)

    def fhalf(d, h):
        return smf.at[lax.rem(p.y + (d + 4), 4), h * 64 : h * 64 + 64]

    def fsend(d, h, peer):
        send(
            lambda: (
                fhalf(d, h), fhalf(d, h), tysem.at[lax.rem(p.y + (d + 4), 4), h], peer
            )
        )

    def fgot(d, h):
        arrived(fhalf(d, h), tysem.at[lax.rem(p.y + (d + 4), 4), h])

    stm[...] = jnp.full_like(stm, -1e30)
    stl[...] = jnp.zeros_like(stl)
    stu[...] = jnp.zeros_like(stu)

    def stats(j):
        kj = kv[pl.ds(j * 2, 2), :, :HD].reshape(256, HD)
        vj = kv[pl.ds(j * 2, 2), :, HD:].reshape(256, HD)
        k_index = row + j * 256
        allowed = (k_index <= q_index) & (k_index >= first)
        for n in range(chunks):
            cols = slice(n * width, (n + 1) * width)
            m = stm[:, cols]
            s = jnp.dot(kj, qt[:, cols], preferred_element_type=F32) * (SCALE * LOG2E)
            s = jnp.where(allowed, s, -1e30)
            d = jnp.dot(vj, dot_t[:, cols], preferred_element_type=F32)
            scr[j, :, cols] = s
            dpr[j, :, cols] = d
            m_new = jnp.maximum(m, jnp.max(s, axis=0, keepdims=True))
            e = jnp.where(allowed, jnp.exp2(s - m_new), 0.0)
            fix = jnp.exp2(m - m_new)
            stm[:, cols] = m_new
            stl[:, cols] = stl[:, cols] * fix + jnp.sum(e, axis=0, keepdims=True)
            stu[:, cols] = stu[:, cols] * fix + jnp.sum(e * d, axis=0, keepdims=True)

    def group_step(g, _):
        @pl.when(g == 0)
        def _():
            for k in (1, 3, 2):
                kgot(0, k)
                ksend(0, k, to_right)
                ksend(0, k, to_left)

        @pl.when(g == 1)
        def _():
            for k in (0, 1, 3, 2):
                kgot(-1, k)
                if k in (0, 2):
                    ksend(-1, k, to_right)
                kgot(1, k)
                if k in (1, 3):
                    ksend(1, k, to_left)
            for dx in range(4):
                for k in range(4):
                    if dx or k:
                        token_send(dx, k)

        @pl.when(g == 3)
        def _():
            for k in (0, 1, 3, 2):
                kgot(2, k)

        d = g + lax.div(g, 2) - 2 * lax.div(g, 3)

        def pair_step(r, _):
            j = lax.rem(p.x + d, 4) * 2 + r

            @pl.when(j * 2 <= p.ctx)
            def _():
                stats(j)

            return 0

        return lax.fori_loop(0, 2, pair_step, 0)

    lax.fori_loop(0, 4, group_step, 0)

    shift = [stm[:, n * width : (n + 1) * width] for n in range(chunks)]
    delta = []
    for n in range(chunks):
        cols = slice(n * width, (n + 1) * width)
        shift[n] = shift[n] + jnp.log2(stl[:, cols])
        delta.append(stu[:, cols] / stl[:, cols])
    for n in range(chunks):
        cols = slice(n * width, (n + 1) * width)
        stm[:, cols] = shift[n]
        stu[:, cols] = delta[n]
    dq[...] = jnp.zeros_like(dq)

    def acopy(t):
        peer = p.mix(p.xn(1), p.xn(-1), lax.rem(t, 2))
        return pltpu.make_async_remote_copy(
            src_ref=a_st.at[t],
            dst_ref=a_rb.at[t],
            send_sem=asend.at[t],
            recv_sem=asem.at[t],
            device_id=peer,
            device_id_type=MESH,
        )

    def grads(t, _):
        q, r = lax.div(t, 2), lax.rem(t, 2)
        middle = lax.div(q * (3 - q), 2)
        d = middle * (1 + 2 * r) + (1 - middle) * lax.div((3 - q) * 2, 3)
        flip = middle * (2 - q)
        h = r + flip * (1 - 2 * r)
        j = lax.rem(p.x + d, 4) * 2 + h

        @pl.when(j * 2 <= p.ctx)
        def _():
            kj = kv[pl.ds(j * 2, 2), :, :HD].reshape(256, HD)
            kt = kj.astype(F32).T.astype(BF)
            dk = jnp.zeros((256, HD), F32)
            dv = jnp.zeros((256, HD), F32)
            for n in range(chunks):
                cols = slice(n * width, (n + 1) * width)
                prob = jnp.exp2(scr[j, :, cols] - stm[:, cols])
                ds = (prob * (dpr[j, :, cols] - stu[:, cols])).astype(BF)
                dv += jnp.dot(prob.astype(BF), do[cols, :], preferred_element_type=F32)
                dk += jnp.dot(ds, qr[cols, :], preferred_element_type=F32)
                dq[:, cols] += jnp.dot(kt, ds, preferred_element_type=F32)
            a_st[t, :, :, :HD] = (dk * SCALE).astype(BF).reshape(2, 128, HD)
            a_st[t, :, :, HD:] = dv.astype(BF).reshape(2, 128, HD)

        @pl.when(j * 2 > p.ctx)
        def _():
            a_st[t] = jnp.zeros((2, 128, 2 * HD), BF)

        @pl.when(t == 4)
        def _():
            for dx in range(4):
                for k in range(4):
                    if dx or k:
                        source = kslot(dx, k)
                        cols = pl.ds(pl.multiple_of(source * 128, 128), 128)
                        arrived(smf.at[p.y, :, cols], tsem.at[source])
            for h in (0, 1):
                fsend(0, h, yr)
                fsend(0, 1 - h, yl)

        @pl.when(q == 2)
        def _():
            arrived(a_rb.at[t - 4], asem.at[t - 4])
            a_st[t] = (a_st[t].astype(F32) + a_rb[t - 4].astype(F32)).astype(BF)

        @pl.when(t < 6)
        def _():
            acopy(t).start()

        return 0

    lax.fori_loop(0, 8, grads, 0)

    for g in range(groups):
        cols = slice(g * 128, (g + 1) * 128)
        t = dq[:, cols].T * SCALE
        gq[:, cols] = t * cos[...] - pltpu.roll(t, HD // 2, 1) * sin[...]
    stores = [pltpu.make_async_copy(gq, gq_o, osem.at[0])]
    stores[0].start()

    for t in (2, 3, 4, 5):
        arrived(a_rb.at[t], asem.at[t])
    for h, (near, run) in enumerate(((3, 4), (2, 5))):
        total = a_st[6 + h].astype(F32) + a_rb[near].astype(F32) + a_rb[run].astype(F32)
        a_t[h * 2 : h * 2 + 2] = total
        a_zs[h * 2 : h * 2 + 2] = total.astype(BF)
    for k in (2, 1, 3):
        send(
            functools.partial(
                lambda k: (
                    a_zs.at[lax.rem(p.zl + k, 4)], a_z.at[k - 1], azsem.at[k - 1], p.zline(k)
                ),
                k,
            )
        )
    d_kv = a_t[p.zl]
    for k in (1, 3, 2):
        arrived(a_z.at[k - 1], azsem.at[k - 1])
        d_kv += a_z[k - 1].astype(F32)
    dk = d_kv[:, :HD]
    dk = dk * cos[...] - pltpu.roll(dk, HD // 2, 1) * sin[...]
    g = jnp.concatenate([dk, d_kv[:, HD:]], axis=1).astype(BF)

    gall[p.ctx] = g

    def gsend(d, k, peer):
        ksend(d, k, peer, gall, gsem)

    def ggot(d, k):
        kgot(d, k, gall, gsem)

    gsend(0, 0, to_right)
    gsend(0, 0, to_left)
    for k in (2, 1, 3):
        gsend(0, 0, functools.partial(p.zline, k))

    def dgrad(d, h):
        blk = lax.rem(p.y + (d + 4), 4) * 16 + h * 8
        out = []
        for i in range(4):
            wb = wbuf[pl.ds(blk + i * 2, 2)].reshape(256, 256)
            out.append(
                lax.dot_general(g, wb, (((1,), (1,)), ((), ())), preferred_element_type=F32)
            )
        return out

    def dstore(k, d, h, extra=None):
        for i, piece in enumerate(dgrad(d, h)):
            cols = slice(i * 256, (i + 1) * 256)
            if extra is not None:
                piece = piece + extra[:, cols].astype(F32)
            y_s[k, h, :, cols] = piece.astype(BF)

    fgot(-1, 0)
    fsend(-1, 0, yr)
    fgot(1, 1)
    fsend(1, 1, yl)

    dstore(0, 2, 0)
    send(lambda: (y_s.at[0, 0], y_r1.at[0], y1sem.at[0], yr))
    for k in (1, 3, 2):
        ggot(0, k)
        gsend(0, k, to_right)
        gsend(0, k, to_left)
    ggot(-1, 0)
    gsend(-1, 0, to_right)
    ggot(1, 1)
    gsend(1, 1, to_left)
    dstore(0, 2, 1)
    send(lambda: (y_s.at[0, 1], y_r1.at[1], y1sem.at[1], yl))
    ggot(-1, 2)
    gsend(-1, 2, to_right)
    ggot(1, 3)
    gsend(1, 3, to_left)
    dstore(1, 1, 1)
    send(lambda: (y_s.at[1, 1], y_r2.at[0, 1], y2sem.at[1], yr))
    dstore(2, -1, 0)
    send(lambda: (y_s.at[2, 0], y_r2.at[1, 0], y2sem.at[2], yl))
    for k in (1, 3):
        ggot(-1, k)
    for k in (0, 2):
        ggot(1, k)
    for k in (0, 1, 3, 2):
        ggot(2, k)
    for d, h in ((-1, 1), (1, 0), (2, 0), (2, 1)):
        fgot(d, h)

    g_tokens = gall[...].reshape(2048, 256)

    def wgrad(q):
        return jnp.dot(smf[q], g_tokens, preferred_element_type=F32)

    for i in (0, 1):
        q = (1 - c) * 2 + i
        rows = pl.ds(pl.multiple_of(q * 128, 128), 128)
        value = wgrad(q)
        hs[i] = value.astype(BF)
        wg[rows, :] = value
    send(lambda: (hs, hr, fsem.at[0], sib))
    for i in (0, 1):
        q = c * 2 + i
        rows = pl.ds(pl.multiple_of(q * 128, 128), 128)
        wg[rows, :] = wgrad(q)
    vec = []
    for q in range(4):
        rows = slice(q * 128, (q + 1) * 128)
        t = wg[rows, :] * cb[rows, :]
        t = t[:, :HD] + t[:, HD:]
        vec.append(jnp.sum(t.T, axis=0, keepdims=True))
    yv[p.y] = jnp.concatenate(vec + vec, axis=0)
    for k in (2, 1, 3):
        send(functools.partial(lambda k: (yv.at[p.y], yv.at[p.y], vsem.at[k - 1], p.yn(k)), k))
    arrived(hr, fsem.at[0])
    for i in (0, 1):
        rows = pl.ds(pl.multiple_of((c * 2 + i) * 128, 128), 128)
        fs[i] = (wg[rows, :] + hr[i].astype(F32)).astype(BF)
    far_id = p.far(0)
    send(lambda: (fs, fr, fsem.at[1], far_id))

    for k in (1, 3, 2):
        arrived(yv.at[lax.rem(p.y + (4 - k), 4)], vsem.at[k - 1])
    vp[0] = (yv[0] + yv[1]) + (yv[2] + yv[3])
    send(lambda: (vp.at[0], vp.at[1], vpsem.at[0], sib))
    arrived(vp.at[1], vpsem.at[0])
    vp[2] = vp[0] + vp[1]
    send(lambda: (vp.at[2], vp.at[3], vpsem.at[1], far_id))

    arrived(y_r1.at[0], y1sem.at[0])
    dstore(1, 1, 0, y_r1.at[0])
    send(lambda: (y_s.at[1, 0], y_r2.at[0, 0], y2sem.at[0], yr))
    arrived(y_r1.at[1], y1sem.at[1])
    dstore(2, -1, 1, y_r1.at[1])
    send(lambda: (y_s.at[2, 1], y_r2.at[1, 1], y2sem.at[3], yl))

    arrived(vp.at[3], vpsem.at[1])
    own_v = p.zl * 4 + p.x
    gs[own_v] = vp[2] + vp[3]
    for k in (2, 1, 3):
        send(
            functools.partial(
                lambda k: (gs.at[own_v], gs.at[own_v], gxsem.at[k - 1], p.xn(k)), k
            )
        )
    arrived(fr, fsem.at[1])
    fb[pl.ds(c * 2, 2)] = (fs[...].astype(F32) + fr[...].astype(F32)).astype(BF)
    send(lambda: (fb.at[pl.ds(c * 2, 2)], fb.at[pl.ds(c * 2, 2)], fsem.at[2], sib))
    for k in (1, 3, 2):
        arrived(gs.at[p.zl * 4 + lax.rem(p.x + (4 - k), 4)], gxsem.at[k - 1])
    for i, k in enumerate((2, 1, -1)):
        send(
            functools.partial(
                lambda i, k: (
                    gs.at[pl.ds(p.zl * 4, 4)], gs.at[pl.ds(p.zl * 4, 4)], gzsem.at[i], p.zn(k)
                ),
                i, k,
            )
        )
    inv_cols = inv[:, pl.ds(pl.multiple_of(p.y * 2048, 2048), 2048)]
    for h in (0, 1):
        for i, piece in enumerate(dgrad(0, h)):
            dcol[:, h * 1024 + i * 256 : h * 1024 + (i + 1) * 256] = piece
    for i, (s, h) in ((1, (0, 1)), (2, (1, 0)), (0, (0, 0)), (3, (1, 1))):
        arrived(y_r2.at[s, h], y2sem.at[i])
    for h in (0, 1):
        cols = slice(h * 1024, (h + 1) * 1024)
        total = dcol[:, cols] + y_r2[0, h].astype(F32) + y_r2[1, h].astype(F32)
        dcol[:, cols] = total * inv_cols[:, cols]
    stores.append(pltpu.make_async_copy(dcol, gh_o, osem.at[1]))
    stores[-1].start()

    arrived(fb.at[pl.ds((1 - c) * 2, 2)], fsem.at[2])
    for q in range(4):
        rows = slice(q * 128, (q + 1) * 128)
        f = fb[q].astype(F32)
        o = f * ss[rows, :]
        gkw[rows, :] = o[:, :HD]
        gvw[rows, :] = o[:, HD:]
        o = jnp.sum(f * st[rows, :], axis=0, keepdims=True)
        gks[q : q + 1, :] = o[:, :HD]
        gvs[q : q + 1, :] = o[:, HD:]
    for i, (src, dst) in enumerate(((gkw, gkw_o), (gvw, gvw_o), (gks, gks_o), (gvs, gvs_o))):
        stores.append(pltpu.make_async_copy(src, dst, osem.at[2 + i]))
        stores[-1].start()

    for i, k in enumerate((2, 1, -1)):
        zl = lax.rem(p.zl + (4 - k), 4)
        arrived(gs.at[pl.ds(zl * 4, 4)], gzsem.at[i])
    for i in range(16):
        gsm[i * 4 : i * 4 + 4, :] = gs[(i % 4) * 4 + i // 4, :4, :]
    stores.append(pltpu.make_async_copy(gsm, gsm_o, osem.at[6]))
    stores[-1].start()

    send.drain()
    for t in range(6):
        acopy(t).wait_send()
    for store in stores:
        store.wait()


def main_call(*args):
    rows = args[2].shape[1]
    outs = (
        ((128, 2048), F32), ((128, rows), F32), ((512, 128), F32), ((512, 128), F32),
        ((4, 128), F32), ((4, 128), F32), ((64, 128), F32),
    )
    scratch = [pltpu.VMEM(a.shape, a.dtype) for a in args]
    scratch += [pltpu.VMEM(*s) for s in (
        ((128, 128), F32), ((128, 128), F32), ((1, 8192), F32),
        ((512, 256), F32), ((512, 256), F32), ((512, 256), F32),
        ((64, 128, 256), BF), ((32, 128, 256), BF), ((64, 128, 128), BF),
        ((4, 128, 2048), BF), ((128, 256), F32), ((16, 128, 256), BF), ((16, 128, 256), BF),
        ((rows, HD), BF), ((HD, rows), BF), ((rows, HD), BF), ((HD, rows), BF),
        ((8, 256, rows), F32), ((8, 256, rows), F32), ((HD, rows), F32),
        ((1, rows), F32), ((1, rows), F32), ((1, rows), F32),
        ((8, 2, 128, 256), BF), ((6, 2, 128, 256), BF), ((4, 128, 256), F32),
        ((4, 128, 256), BF), ((3, 128, 256), BF),
        ((512, 256), F32), ((2, 128, 256), BF), ((2, 128, 256), BF), ((2, 128, 256), BF),
        ((2, 128, 256), BF), ((4, 128, 256), BF),
        ((3, 2, 128, 1024), BF), ((2, 128, 1024), BF), ((2, 2, 128, 1024), BF),
        ((4, 8, 128), F32), ((4, 8, 128), F32), ((16, 8, 128), F32),
    )]
    scratch += [pltpu.VMEM(*o) for o in outs]
    scratch += [DMA(s) for s in (
        (160,), (10,), (7,), (32,), (16,), (16,), (16,), (16,), (4, 2), (6,), (6,), (3,),
        (3,), (2,), (4,), (3,), (2,), (3,), (3,),
    )]
    return pl.pallas_call(
        main_kernel,
        name="main",
        out_shape=tuple(jax.ShapeDtypeStruct(*o) for o in outs),
        in_specs=[ANY] * len(args),
        out_specs=(ANY,) * len(outs),
        scratch_shapes=scratch,
        compiler_params=pltpu.CompilerParams(
            collective_id=0, has_side_effects=True, vmem_limit_bytes=60 << 20
        ),
    )(*args)


def finish_kernel(*refs):
    count = (len(refs) - 1) // 3
    sems = refs[-1]
    loads, stores = [], []
    for i in range(count):
        held = refs[2 * count + i]
        loads.append(pltpu.make_async_copy(refs[i], held, sems.at[0, i]))
        stores.append(pltpu.make_async_copy(held, refs[count + i], sems.at[1, i]))
    for load in loads:
        load.start()
    for load, store in zip(loads, stores):
        load.wait()
        store.start()
    for store in stores:
        store.wait()


def finish(*arrays):
    return pl.pallas_call(
        finish_kernel,
        name="finish",
        out_shape=tuple(jax.ShapeDtypeStruct(a.shape, a.dtype) for a in arrays),
        in_specs=[ANY] * len(arrays),
        out_specs=(ANY,) * len(arrays),
        scratch_shapes=[pltpu.VMEM(a.shape, a.dtype) for a in arrays] + [DMA((2, len(arrays)))],
        compiler_params=pltpu.CompilerParams(vmem_limit_bytes=60 << 20),
    )(*arrays)


def body(
    hidden_states,
    positions,
    queries,
    key_weight,
    value_weight,
    key_step,
    value_step,
    smoothing,
    grad_out,
):
    index = np.arange(HD) % (HD // 2)
    freq = jnp.asarray((10000.0 ** (-2.0 * index / HD)).astype(np.float32))[None, :]
    gh, gq, gkw, gvw, gks, gvs, gsm = finish(
        *main_call(
            hidden_states[0], positions, queries[0], key_weight, value_weight, key_step,
            value_step, smoothing[None, :], grad_out[0], freq,
        )
    )
    return gh[None], gq[None], gkw, gvw, gks, gvs, gsm.reshape(smoothing.shape)


def solution(mesh):
    in_specs = (
        P("dp", "ctx", None),
        P("dp", "ctx"),
        P("dp", "ctx", "tensor"),
        P("ctx", "tensor"),
        P("ctx", "tensor"),
        P("ctx", "tensor"),
        P("ctx", "tensor"),
        P(),
        P("dp", "ctx", "tensor"),
    )
    out_specs = (
        P("dp", "ctx", "tensor"),
        P("dp", "ctx", "tensor"),
        P("ctx", "tensor"),
        P("ctx", "tensor"),
        P("ctx", "tensor"),
        P("ctx", "tensor"),
        P(),
    )
    return jax.shard_map(body, mesh=mesh, in_specs=in_specs, out_specs=out_specs, check_vma=False)
```

```python
import functools
import math

import jax
import jax.numpy as jnp
import numpy as np
from jax import lax
from jax.experimental import pallas as pl
from jax.experimental.pallas import tpu as pltpu
from jax.sharding import PartitionSpec as P

HD = 128
GROUP = 128
TWO_PI = 2.0 * math.pi
LOG2E = 1.4426950408889634
SCALE = HD ** (-0.5)
MESH = pl.DeviceIdType.MESH
BF = jnp.bfloat16
F32 = jnp.float32
ANY = pl.BlockSpec(memory_space=pl.ANY)
DMA = pltpu.SemaphoreType.DMA
ZOFFSETS = (4, 3, -3, 2, -2, 1, -1)
VPEERS = ((2, 1), (1, 1), (3, 1), (2, 0), (1, 0), (3, 0), (0, 1))


class Place:
    def __init__(self):
        self.ctx = lax.axis_index("ctx")
        self.dp = lax.axis_index("dp")
        self.y = lax.axis_index("tensor")
        self.x = lax.div(self.ctx, 4)
        self.zl = lax.rem(self.ctx, 4)
        self.zh = lax.div(self.dp, 2)
        self.c = lax.rem(self.dp, 2)
        self.z = self.zh * 4 + self.zl

        self.X = [self.x] + [lax.rem(self.x + d, 4) for d in (1, 2, 3)]
        self.L = [self.zl] + [lax.rem(self.zl + d, 4) for d in (1, 2, 3)]
        self.Y = [self.y] + [lax.rem(self.y + d, 4) for d in (1, 2, 3)]
        self.Z = {}
        for d in (1, -1, 2, -2, 3, -3, 4):
            z = lax.rem(self.z + (d + 8), 8)
            self.Z[d] = (self.x * 4 + self.L[d % 4], lax.div(z, 4) * 2 + self.c)
        self.sibling = self.zh * 2 + (1 - self.c)

    def xn(self, d):
        return {"ctx": self.X[d % 4] * 4 + self.zl, "dp": self.dp}

    def zn(self, d):
        return {"ctx": self.Z[d][0], "dp": self.Z[d][1]}

    def at(self, dx, k):
        return {"ctx": self.X[dx % 4] * 4 + self.L[k % 4], "dp": self.dp}

    def zline(self, d):
        return {"ctx": self.x * 4 + self.L[d], "dp": self.dp}

    def yn(self, d):
        return {"tensor": self.Y[d % 4]}

    def ys(self, k, other):
        return {"tensor": self.Y[k], "dp": self.sibling if other else self.dp}

    def sib(self):
        return {"dp": self.sibling}

    def far(self, other):
        c = (1 - self.c) if other else self.c
        return {"dp": (1 - self.zh) * 2 + c}

    def mix(self, first, second, c):
        return {k: first[k] * (1 - c) + second[k] * c for k in first}


class Sender:
    def __init__(self, sems):
        self.sems = sems
        self.used = 0
        self.sent = []

    def make(self, index, what):
        src, dst, recv, peer = what()
        return pltpu.make_async_remote_copy(
            src_ref=src,
            dst_ref=dst,
            send_sem=self.sems.at[index],
            recv_sem=recv,
            device_id=peer,
            device_id_type=MESH,
        )

    def __call__(self, what):
        index = self.used
        self.used += 1
        self.sent.append((index, what))
        self.make(index, what).start()

    def drain(self):
        for index, what in self.sent:
            self.make(index, what).wait_send()
        self.sent = []


def arrived(ref, sem):
    pltpu.make_async_copy(ref, ref, sem).wait()


def sin_cos_turns(r):
    t = (r - jnp.floor(r + 0.5)) * TWO_PI
    q = t * t
    s = jnp.full_like(t, 1.0)
    for n in (14, 12, 10, 8, 6, 4, 2):
        s = 1.0 - q * s * (1.0 / (n * (n + 1)))
    k = jnp.full_like(t, 1.0)
    for n in (15, 13, 11, 9, 7, 5, 3, 1):
        k = 1.0 - q * k * (1.0 / (n * (n + 1)))
    return s * t, k


def spread(row):
    return jnp.broadcast_to(row, (128, row.shape[1])).T


def main_kernel(
    hid_h, pos_h, q_h, kw_h, vw_h, ks_h, vs_h, smooth_h, do_h, freq_h,
    gh_o, gq_o, gkw_o, gvw_o, gks_o, gvs_o, gsm_o,
    hid, pos, queries, kw, vw, ks, vs, smooth, dout, freq,
    cos, sin, inv, ss, st, cb,
    wbuf, sm, smt, smf, acc, kv, gall,
    qr, qt, do, dot_t, scr, dpr, dq, stm, stl, stu,
    a_st, a_rb, a_t, a_zs, a_z,
    wg, hs, hr, fs, fr, fb,
    y_s, y_r1, y_r2, yv, gs,
    dcol, gq, gkw, gvw, gks, gvs, gsm,
    ssem, csem, osem, nsem, sibsem, kvsem, gsem, tsem, tysem, asem, asend, azsem,
    fsem, y1sem, y2sem, vsem, gxsem, gzsem,
):
    p = Place()
    c = p.c
    pairs = (
        (kw_h, kw), (vw_h, vw), (ks_h, ks), (vs_h, vs), (smooth_h, smooth),
        (pos_h, pos), (freq_h, freq), (hid_h, hid), (q_h, queries), (do_h, dout),
    )
    loads = [pltpu.make_async_copy(s, d, csem.at[i]) for i, (s, d) in enumerate(pairs)]
    for load in loads:
        load.start()
    xr, xl, yr, yl, sib = p.xn(1), p.xn(-1), p.yn(1), p.yn(-1), p.sib()
    peers = [yr, yl, p.yn(2), sib] + [p.zn(k) for k in (1, -1, 2, -2, 3, -3, 4)]
    peers += [p.ys(k, 1) for k in (1, 2, 3)]
    peers += [p.at(dx, k) for dx in range(4) for k in range(4) if dx or k]
    barrier = pltpu.get_barrier_semaphore()
    for peer in peers:
        pl.semaphore_signal(barrier, inc=1, device_id=peer, device_id_type=MESH)
    send = Sender(ssem)

    slots = {}
    for a in range(4):
        for b in range(4):
            slots[a, b] = (p.X[a] * 4 + p.L[b]) * (1 - c) + (p.X[b] * 4 + p.L[a]) * c

    def slot(a, b):
        return slots[a % 4, b % 4]

    own = slot(0, 0)
    for load in loads[:5]:
        load.wait()

    def quantize(q):
        rows = pl.ds(pl.multiple_of(q * 128, 128), 128)
        s_row = smooth[:, pl.ds(pl.multiple_of(p.ctx * 512 + q * 128, 128), 128)]
        s_col = spread(s_row)
        for half, (w_ref, step_ref) in enumerate(((kw, ks), (vw, vs))):
            cols = slice(half * HD, (half + 1) * HD)
            weight = w_ref[rows, :].astype(F32)
            step = step_ref[pl.ds(q, 1), :]
            ratio = weight * s_col / step
            sine, cosine = sin_cos_turns(ratio)
            sine = sine * (1.0 / TWO_PI)
            quant = (step * (ratio - sine)).astype(BF)
            wbuf[own * 4 + q, :, cols] = quant
            slope = 1.0 - cosine
            ss[rows, cols] = slope * s_col
            st[rows, cols] = ratio * cosine - sine
            cb[rows, cols] = slope * weight - quant.astype(F32) / s_col

    quantize(c * 2)
    quantize(c * 2 + 1)
    pl.semaphore_wait(barrier, len(peers))

    an = {d: p.mix(p.xn(d), p.zn(d), c) for d in (1, -1)}
    bn = {d: p.mix(p.zn(d), p.xn(d), c) for d in (1, -1)}

    def chunk(s, sub):
        return wbuf.at[s * 4 + c * 2 + sub]

    def net(s, sub, peer):
        send(lambda: (chunk(s, sub), chunk(s, sub), nsem.at[s * 2 + sub], peer))

    def got(s, sub):
        arrived(chunk(s, sub), nsem.at[s * 2 + sub])

    def to_sib(s):
        ref = wbuf.at[pl.ds(s * 4 + c * 2, 2)]
        send(lambda: (ref, ref, sibsem.at[s], sib))

    def from_sib(s):
        arrived(wbuf.at[pl.ds(s * 4 + (1 - c) * 2, 2)], sibsem.at[s])

    def dot(s, h):
        w = wbuf[pl.ds(s * 4 + h * 2, 2)].reshape(256, 256)
        acc[...] += jnp.dot(sm[s * 2 + h], w, preferred_element_type=F32)

    for sub in (0, 1):
        net(own, sub, an[1])
        net(own, 1 - sub, an[-1])
        net(own, sub, bn[1])
        net(own, 1 - sub, bn[-1])

    def prepare(j0, j1):
        for j in range(j0, j1):
            cols = slice(j * 256, (j + 1) * 256)
            block = hid[:, cols].astype(F32) * inv[:, cols]
            sm[j] = block.astype(BF)

    inv[...] = 1.0 / smooth[...]
    left, right, far = slot(-1, 0), slot(1, 0), slot(2, 0)
    got(left, 0)
    net(left, 0, an[1])
    got(right, 1)
    net(right, 1, an[-1])
    for s, sub in ((left, 0), (right, 1)):
        net(s, sub, bn[1])
        net(s, sub, bn[-1])
    quantize((1 - c) * 2)
    quantize((1 - c) * 2 + 1)
    for s, sub in ((left, 1), (right, 0)):
        got(s, sub)
        net(s, sub, bn[1])
        net(s, sub, bn[-1])
        to_sib(s)
    loads[7].wait()
    prepare(0, 6)

    def across(a):
        bl, br = slot(a, -1), slot(a, 1)
        got(bl, 0)
        net(bl, 0, bn[1])
        got(br, 1)
        net(br, 1, bn[-1])
        got(bl, 1)
        got(br, 0)
        to_sib(bl)
        to_sib(br)
        return bl, br

    ready = [*across(0), left, right]
    for sub in (0, 1):
        got(far, sub)
        net(far, sub, bn[1])
        net(far, sub, bn[-1])
    to_sib(far)
    ready.append(far)
    prepare(6, 24)
    for load in loads[5:7]:
        load.wait()
    angle = spread(pos[...].astype(F32)) * freq[...]
    cos[...] = jnp.cos(angle)
    turned = jnp.sin(angle)
    lane = lax.broadcasted_iota(jnp.int32, (128, 128), 1)
    sin[...] = jnp.where(lane < HD // 2, -turned, turned)

    ready += across(-1)
    prepare(24, 32)
    groups = qr.shape[0] // 128
    for load in loads[8:]:
        load.wait()
    for g in range(groups):
        cols = slice(g * 128, (g + 1) * 128)
        q = queries[:, cols].astype(F32)
        q = q * cos[...] + pltpu.roll(q, HD // 2, 1) * sin[...]
        qr[cols, :] = q.astype(BF)
        qt[:, cols] = q.T.astype(BF)
        d = dout[:, cols]
        do[cols, :] = d
        dot_t[:, cols] = d.astype(F32).T.astype(BF)
    acc[...] = jnp.zeros_like(acc)
    dot(own, 0)
    dot(own, 1)
    ready += across(1)

    for s in ready[:5]:
        dot(s, c)
    ready += across(2)
    for s in ready[5:]:
        dot(s, c)
    for a in (-1, 1, 0, 2):
        for b in (0, -1, 1):
            if a == 0 and b == 0:
                continue
            s = slot(b, a)
            from_sib(s)
            dot(s, 1 - c)
    for a in (0, -1, 1, 2):
        s = slot(a, 2)
        got(s, 0)
        got(s, 1)
        to_sib(s)
        dot(s, c)
    for a in (-1, 1, 0, 2):
        s = slot(2, a)
        from_sib(s)
        dot(s, 1 - c)

    key_raw = acc[:, :HD]
    rotated = key_raw * cos[...] + pltpu.roll(key_raw, HD // 2, 1) * sin[...]
    kv[p.ctx, :, :HD] = rotated.astype(BF)
    kv[p.ctx, :, HD:] = acc[:, HD:].astype(BF)

    def kslot(d, k):
        return p.X[d % 4] * 4 + p.L[k % 4]

    def ksend(d, k, peer, buf=kv, sem=kvsem):
        def what():
            s = kslot(d, k)
            return buf.at[s], buf.at[s], sem.at[s], peer()

        send(what)

    def kgot(d, k, buf=kv, sem=kvsem):
        s = kslot(d, k)
        arrived(buf.at[s], sem.at[s])

    to_right, to_left = (lambda: p.xn(1)), (lambda: p.xn(-1))
    ksend(0, 0, to_right)
    ksend(0, 0, to_left)
    for k in (2, 1, 3):
        ksend(0, 0, functools.partial(p.zline, k))

    for j in range(32):
        smt[j * 2 : j * 2 + 2] = sm[j].astype(F32).T.astype(BF).reshape(2, 128, 128)
    smf[p.y, :, pl.ds(pl.multiple_of(p.ctx * 128, 128), 128)] = smt[p.ctx * 4 + p.y]
    width = 256
    chunks = qr.shape[0] // width
    q_index = p.ctx * 128 + lax.rem(lax.broadcasted_iota(jnp.int32, (1, width), 1), 128)
    first = q_index - jnp.concatenate([pos[...]] * (width // 128), axis=1)
    row = lax.broadcasted_iota(jnp.int32, (256, width), 0)
    def token_send(dx, k):
        def what():
            dest = p.X[dx] * 4 + p.L[k]
            cols = pl.ds(pl.multiple_of(p.ctx * 128, 128), 128)
            return smt.at[dest * 4 + p.y], smf.at[p.y, :, cols], tsem.at[p.ctx], p.at(dx, k)

        send(what)

    def fhalf(d, h):
        return smf.at[p.Y[d % 4], h * 64 : h * 64 + 64]

    def fsend(d, h, peer):
        send(
            lambda: (
                fhalf(d, h), fhalf(d, h), tysem.at[p.Y[d % 4], h], peer
            )
        )

    def fgot(d, h):
        arrived(fhalf(d, h), tysem.at[p.Y[d % 4], h])

    stm[...] = jnp.full_like(stm, -1e30)
    stl[...] = jnp.zeros_like(stl)
    stu[...] = jnp.zeros_like(stu)

    def stats(j):
        kj = kv[pl.ds(j * 2, 2), :, :HD].reshape(256, HD)
        vj = kv[pl.ds(j * 2, 2), :, HD:].reshape(256, HD)
        k_index = row + j * 256
        allowed = (k_index <= q_index) & (k_index >= first)
        for n in range(chunks):
            cols = slice(n * width, (n + 1) * width)
            m = stm[:, cols]
            s = jnp.dot(kj, qt[:, cols], preferred_element_type=F32) * (SCALE * LOG2E)
            s = jnp.where(allowed, s, -1e30)
            d = jnp.dot(vj, dot_t[:, cols], preferred_element_type=F32)
            scr[j, :, cols] = s
            dpr[j, :, cols] = d
            m_new = jnp.maximum(m, jnp.max(s, axis=0, keepdims=True))
            e = jnp.where(allowed, jnp.exp2(s - m_new), 0.0)
            fix = jnp.exp2(m - m_new)
            stm[:, cols] = m_new
            stl[:, cols] = stl[:, cols] * fix + jnp.sum(e, axis=0, keepdims=True)
            stu[:, cols] = stu[:, cols] * fix + jnp.sum(e * d, axis=0, keepdims=True)

    def group_step(g, _):
        @pl.when(g == 0)
        def _():
            for k in (1, 3, 2):
                kgot(0, k)
                ksend(0, k, to_right)
                ksend(0, k, to_left)

        @pl.when(g == 1)
        def _():
            for k in (0, 1, 3, 2):
                kgot(-1, k)
                if k in (0, 2):
                    ksend(-1, k, to_right)
                kgot(1, k)
                if k in (1, 3):
                    ksend(1, k, to_left)
            for dx in range(4):
                for k in range(4):
                    if dx or k:
                        token_send(dx, k)

        @pl.when(g == 3)
        def _():
            for k in (0, 1, 3, 2):
                kgot(2, k)

        d = g + lax.div(g, 2) - 2 * lax.div(g, 3)

        def pair_step(r, _):
            j = lax.rem(p.x + d, 4) * 2 + r

            @pl.when(j * 2 <= p.ctx)
            def _():
                stats(j)

            return 0

        return lax.fori_loop(0, 2, pair_step, 0)

    lax.fori_loop(0, 4, group_step, 0)

    shift = [stm[:, n * width : (n + 1) * width] for n in range(chunks)]
    delta = []
    for n in range(chunks):
        cols = slice(n * width, (n + 1) * width)
        shift[n] = shift[n] + jnp.log2(stl[:, cols])
        delta.append(stu[:, cols] / stl[:, cols])
    for n in range(chunks):
        cols = slice(n * width, (n + 1) * width)
        stm[:, cols] = shift[n]
        stu[:, cols] = delta[n]
    dq[...] = jnp.zeros_like(dq)

    def acopy(v, t):
        peer = p.mix(p.xn(1), p.xn(-1), lax.rem(t, 2))
        return pltpu.make_async_remote_copy(
            src_ref=a_st.at[v, t],
            dst_ref=a_rb.at[v, t],
            send_sem=asend.at[v, t],
            recv_sem=asem.at[v, t],
            device_id=peer,
            device_id_type=MESH,
        )

    def grads(t, _):
        q, r = lax.div(t, 2), lax.rem(t, 2)
        middle = lax.div(q * (3 - q), 2)
        d = middle * (1 + 2 * r) + (1 - middle) * lax.div((3 - q) * 2, 3)
        flip = middle * (2 - q)
        h = r + flip * (1 - 2 * r)
        j = lax.rem(p.x + d, 4) * 2 + h

        @pl.when(j * 2 <= p.ctx)
        def _():
            kj = kv[pl.ds(j * 2, 2), :, :HD].reshape(256, HD)
            kt = kj.astype(F32).T.astype(BF)
            dk = jnp.zeros((256, HD), F32)
            dv = jnp.zeros((256, HD), F32)
            for n in range(chunks):
                cols = slice(n * width, (n + 1) * width)
                prob = jnp.exp2(scr[j, :, cols] - stm[:, cols])
                ds = (prob * (dpr[j, :, cols] - stu[:, cols])).astype(BF)
                dv += jnp.dot(prob.astype(BF), do[cols, :], preferred_element_type=F32)
                dk += jnp.dot(ds, qr[cols, :], preferred_element_type=F32)
                dq[:, cols] += jnp.dot(kt, ds, preferred_element_type=F32)
            a_st[0, t] = (dk * SCALE).astype(BF).reshape(2, 128, HD)
            a_st[1, t] = dv.astype(BF).reshape(2, 128, HD)

        @pl.when(j * 2 > p.ctx)
        def _():
            a_st[0, t] = jnp.zeros((2, 128, HD), BF)
            a_st[1, t] = jnp.zeros((2, 128, HD), BF)

        @pl.when(t == 4)
        def _():
            for dx in range(4):
                for k in range(4):
                    if dx or k:
                        source = kslot(dx, k)
                        cols = pl.ds(pl.multiple_of(source * 128, 128), 128)
                        arrived(smf.at[p.y, :, cols], tsem.at[source])
            for h in (0, 1):
                fsend(0, h, yr)
                fsend(0, 1 - h, yl)

        @pl.when(q == 2)
        def _():
            for v in (0, 1):
                arrived(a_rb.at[v, t - 4], asem.at[v, t - 4])
                total = a_st[v, t].astype(F32) + a_rb[v, t - 4].astype(F32)
                a_st[v, t] = total.astype(BF)
                acopy(v, t).start()

        @pl.when(t < 4)
        def _():
            acopy(0, t).start()
            acopy(1, t).start()

        return 0

    lax.fori_loop(0, 8, grads, 0)

    for v in (0, 1):
        for t in (2, 3, 4, 5):
            arrived(a_rb.at[v, t], asem.at[v, t])
        for h, (near, run) in enumerate(((3, 4), (2, 5))):
            total = a_st[v, 6 + h].astype(F32) + a_rb[v, near].astype(F32)
            total = total + a_rb[v, run].astype(F32)
            a_t[v, h * 2 : h * 2 + 2] = total
            a_zs[v, h * 2 : h * 2 + 2] = total.astype(BF)
        for k in (2, 1, 3):
            send(
                functools.partial(
                    lambda v, k: (
                        a_zs.at[v, p.L[k % 4]], a_z.at[v, k - 1],
                        azsem.at[v, k - 1], p.zline(k),
                    ),
                    v, k,
                )
            )
    for g in range(groups):
        cols = slice(g * 128, (g + 1) * 128)
        t = dq[:, cols].T * SCALE
        gq[:, cols] = t * cos[...] - pltpu.roll(t, HD // 2, 1) * sin[...]
    stores = [pltpu.make_async_copy(gq, gq_o, osem.at[0])]
    stores[0].start()

    def gsend(v, d, k, peer):
        ksend(d, k, peer, gall.at[v], gsem.at[v])

    def ggot(v, d, k):
        kgot(d, k, gall.at[v], gsem.at[v])

    parts = []
    for v in (0, 1):
        total = a_t[v, p.zl]
        for k in (1, 3, 2):
            arrived(a_z.at[v, k - 1], azsem.at[v, k - 1])
            total += a_z[v, k - 1].astype(F32)
        if v == 0:
            total = total * cos[...] - pltpu.roll(total, HD // 2, 1) * sin[...]
        parts.append(total.astype(BF))
        gall[v, p.ctx] = parts[v]
        for k in (2, 1, 3):
            gsend(v, 0, 0, functools.partial(p.zline, k))
        gsend(v, 0, 0, to_right)
        gsend(v, 0, 0, to_left)
    g = jnp.concatenate(parts, axis=1)
    def dgrad(d, h):
        blk = p.Y[d % 4] * 16 + h * 8
        out = []
        for i in range(4):
            wb = wbuf[pl.ds(blk + i * 2, 2)].reshape(256, 256)
            out.append(
                lax.dot_general(g, wb, (((1,), (1,)), ((), ())), preferred_element_type=F32)
            )
        return out

    def dstore(k, d, h, extra=None):
        for i, piece in enumerate(dgrad(d, h)):
            cols = slice(i * 256, (i + 1) * 256)
            if extra is not None:
                piece = piece + extra[:, cols].astype(F32)
            y_s[k, h, :, cols] = piece.astype(BF)

    fgot(-1, 0)
    fsend(-1, 0, yr)
    fgot(1, 1)
    fsend(1, 1, yl)
    dstore(0, 2, 0)
    send(lambda: (y_s.at[0, 0], y_r1.at[0], y1sem.at[0], yr))
    dstore(0, 2, 1)
    send(lambda: (y_s.at[0, 1], y_r1.at[1], y1sem.at[1], yl))

    for v in (0, 1):
        for k in (1, 3, 2):
            ggot(v, 0, k)
            gsend(v, 0, k, to_right)
            gsend(v, 0, k, to_left)
    dstore(1, 1, 1)
    send(lambda: (y_s.at[1, 1], y_r2.at[0, 1], y2sem.at[1], yr))
    for a, b in ((0, 1), (2, 3)):
        if a == 2:
            dstore(2, -1, 0)
            send(lambda: (y_s.at[2, 0], y_r2.at[1, 0], y2sem.at[2], yl))
        for v in (0, 1):
            ggot(v, -1, a)
            gsend(v, -1, a, to_right)
            ggot(v, 1, b)
            gsend(v, 1, b, to_left)
    for d, h in ((-1, 1), (1, 0), (2, 0), (2, 1)):
        fgot(d, h)

    far_id = p.far(0)

    def fcopy(v):
        send(lambda: (fs.at[v], fr.at[v], fsem.at[v, 1], far_id))

    early = len(send.sent)
    vec = [jnp.zeros((1, 128), F32) for _ in range(4)]
    for v in (0, 1):
        for k in (1, 3):
            ggot(v, -1, k)
        for k in (0, 2):
            ggot(v, 1, k)
        for k in (0, 1, 3, 2):
            ggot(v, 2, k)
        tokens = gall[v].reshape(2048, HD)
        for half in (1 - c, c):
            for i in (0, 1):
                q = half * 2 + i
                rows = pl.ds(pl.multiple_of(q * 128, 128), 128)
                value = jnp.dot(smf[q], tokens, preferred_element_type=F32)
                wg[v, rows, :] = value
                if half is not c:
                    hs[v, i] = value.astype(BF)
            if half is not c:
                send(functools.partial(lambda v: (hs.at[v], hr.at[v], fsem.at[v, 0], sib), v))
        cols = slice(v * HD, (v + 1) * HD)
        for q in range(4):
            rows = slice(q * 128, (q + 1) * 128)
            vec[q] += jnp.sum((wg[v, rows, :] * cb[rows, cols]).T, axis=0, keepdims=True)
        if v == 1:
            yv[p.y * 2 + p.c] = jnp.concatenate(vec + vec, axis=0)
            for k, other in VPEERS:
                send(
                    functools.partial(
                        lambda k, other: (
                            yv.at[p.y * 2 + p.c], yv.at[p.y * 2 + p.c],
                            vsem.at[k * 2 + other], p.ys(k, other),
                        ),
                        k, other,
                    )
                )
        arrived(hr.at[v], fsem.at[v, 0])
        for i in (0, 1):
            rows = pl.ds(pl.multiple_of((c * 2 + i) * 128, 128), 128)
            fs[v, i] = (wg[v, rows, :] + hr[v, i].astype(F32)).astype(BF)
        fcopy(v)

    late = send.sent[early:]
    send.sent = send.sent[:early]
    for k, other in VPEERS:
        core = c * (1 - other) + (1 - c) * other
        arrived(yv.at[p.Y[(4 - k) % 4] * 2 + core], vsem.at[k * 2 + other])
    first_sent, send.sent = send.sent, []
    gs[p.z, p.x] = ((yv[0] + yv[1]) + (yv[2] + yv[3])) + ((yv[4] + yv[5]) + (yv[6] + yv[7]))
    for k in (2, 1, 3):
        send(
            functools.partial(
                lambda k: (gs.at[p.z, p.x], gs.at[p.z, p.x], gxsem.at[k - 1], p.xn(k)), k
            )
        )

    arrived(y_r1.at[0], y1sem.at[0])
    dstore(1, 1, 0, y_r1.at[0])
    send(lambda: (y_s.at[1, 0], y_r2.at[0, 0], y2sem.at[0], yr))
    arrived(y_r1.at[1], y1sem.at[1])
    dstore(2, -1, 1, y_r1.at[1])
    send(lambda: (y_s.at[2, 1], y_r2.at[1, 1], y2sem.at[3], yl))

    for k in (1, 3, 2):
        arrived(gs.at[p.z, p.X[4 - k]], gxsem.at[k - 1])
    for k in ZOFFSETS:
        send(
            functools.partial(
                lambda k: (gs.at[p.z], gs.at[p.z], gzsem.at[k + 3], p.zn(k)), k
            )
        )
    tail, send.sent = send.sent, first_sent
    send.drain()
    for v in (0, 1):
        for t in range(6):
            acopy(v, t).wait_send()
    send.sent = late + tail
    for v in (0, 1):
        arrived(fr.at[v], fsem.at[v, 1])
        fb[v, pl.ds(c * 2, 2)] = (fs[v].astype(F32) + fr[v].astype(F32)).astype(BF)
        send(
            functools.partial(
                lambda v: (
                    fb.at[v, pl.ds(c * 2, 2)], fb.at[v, pl.ds(c * 2, 2)], fsem.at[v, 2], sib
                ),
                v,
            )
        )
    inv_cols = inv[:, pl.ds(pl.multiple_of(p.y * 2048, 2048), 2048)]
    for h in (0, 1):
        for i, piece in enumerate(dgrad(0, h)):
            dcol[:, h * 1024 + i * 256 : h * 1024 + (i + 1) * 256] = piece
    for i, (s, h) in ((1, (0, 1)), (2, (1, 0)), (0, (0, 0)), (3, (1, 1))):
        arrived(y_r2.at[s, h], y2sem.at[i])
    for h in (0, 1):
        cols = slice(h * 1024, (h + 1) * 1024)
        total = dcol[:, cols] + y_r2[0, h].astype(F32) + y_r2[1, h].astype(F32)
        dcol[:, cols] = total * inv_cols[:, cols]
    stores.append(pltpu.make_async_copy(dcol, gh_o, osem.at[1]))
    stores[-1].start()

    for v, (weights, totals) in enumerate(((gkw, gks), (gvw, gvs))):
        arrived(fb.at[v, pl.ds((1 - c) * 2, 2)], fsem.at[v, 2])
        cols = slice(v * HD, (v + 1) * HD)
        for q in range(4):
            rows = slice(q * 128, (q + 1) * 128)
            f = fb[v, q].astype(F32)
            weights[rows, :] = f * ss[rows, cols]
            totals[q : q + 1, :] = jnp.sum(f * st[rows, cols], axis=0, keepdims=True)
    for i, (src, dst) in enumerate(((gkw, gkw_o), (gvw, gvw_o), (gks, gks_o), (gvs, gvs_o))):
        stores.append(pltpu.make_async_copy(src, dst, osem.at[2 + i]))
        stores[-1].start()

    for k in ZOFFSETS:
        arrived(gs.at[lax.rem(p.z + (8 - k), 8)], gzsem.at[k + 3])
    for i in range(16):
        zl, x = i % 4, i // 4
        gsm[i * 4 : i * 4 + 4, :] = gs[zl, x, :4, :] + gs[4 + zl, x, :4, :]
    stores.append(pltpu.make_async_copy(gsm, gsm_o, osem.at[6]))
    stores[-1].start()

    send.drain()
    for store in stores:
        store.wait()


def main_call(*args):
    rows = args[2].shape[1]
    outs = (
        ((128, 2048), F32), ((128, rows), F32), ((512, 128), F32), ((512, 128), F32),
        ((4, 128), F32), ((4, 128), F32), ((64, 128), F32),
    )
    scratch = [pltpu.VMEM(a.shape, a.dtype) for a in args]
    scratch += [pltpu.VMEM(*s) for s in (
        ((128, 128), F32), ((128, 128), F32), ((1, 8192), F32),
        ((512, 256), F32), ((512, 256), F32), ((512, 256), F32),
        ((64, 128, 256), BF), ((32, 128, 256), BF), ((64, 128, 128), BF),
        ((4, 128, 2048), BF), ((128, 256), F32), ((16, 128, 256), BF), ((2, 16, 128, 128), BF),
        ((rows, HD), BF), ((HD, rows), BF), ((rows, HD), BF), ((HD, rows), BF),
        ((8, 256, rows), F32), ((8, 256, rows), F32), ((HD, rows), F32),
        ((1, rows), F32), ((1, rows), F32), ((1, rows), F32),
        ((2, 8, 2, 128, 128), BF), ((2, 6, 2, 128, 128), BF), ((2, 4, 128, 128), F32),
        ((2, 4, 128, 128), BF), ((2, 3, 128, 128), BF),
        ((2, 512, 128), F32), ((2, 2, 128, 128), BF), ((2, 2, 128, 128), BF),
        ((2, 2, 128, 128), BF), ((2, 2, 128, 128), BF), ((2, 4, 128, 128), BF),
        ((3, 2, 128, 1024), BF), ((2, 128, 1024), BF), ((2, 2, 128, 1024), BF),
        ((8, 8, 128), F32), ((8, 4, 8, 128), F32),
    )]
    scratch += [pltpu.VMEM(*o) for o in outs]
    scratch += [DMA(s) for s in (
        (192,), (10,), (7,), (32,), (16,), (16,), (2, 16), (16,), (4, 2), (2, 6), (2, 6),
        (2, 3), (2, 3), (2,), (4,), (8,), (3,), (8,),
    )]
    return pl.pallas_call(
        main_kernel,
        name="main",
        out_shape=tuple(jax.ShapeDtypeStruct(*o) for o in outs),
        in_specs=[ANY] * len(args),
        out_specs=(ANY,) * len(outs),
        scratch_shapes=scratch,
        compiler_params=pltpu.CompilerParams(
            collective_id=0, has_side_effects=True, vmem_limit_bytes=60 << 20
        ),
    )(*args)


def finish_kernel(*refs):
    count = (len(refs) - 1) // 3
    sems = refs[-1]
    loads, stores = [], []
    for i in range(count):
        held = refs[2 * count + i]
        loads.append(pltpu.make_async_copy(refs[i], held, sems.at[0, i]))
        stores.append(pltpu.make_async_copy(held, refs[count + i], sems.at[1, i]))
    for load in loads:
        load.start()
    for load, store in zip(loads, stores):
        load.wait()
        store.start()
    for store in stores:
        store.wait()


def finish(*arrays):
    return pl.pallas_call(
        finish_kernel,
        name="finish",
        out_shape=tuple(jax.ShapeDtypeStruct(a.shape, a.dtype) for a in arrays),
        in_specs=[ANY] * len(arrays),
        out_specs=(ANY,) * len(arrays),
        scratch_shapes=[pltpu.VMEM(a.shape, a.dtype) for a in arrays] + [DMA((2, len(arrays)))],
        compiler_params=pltpu.CompilerParams(vmem_limit_bytes=60 << 20),
    )(*arrays)


def body(
    hidden_states,
    positions,
    queries,
    key_weight,
    value_weight,
    key_step,
    value_step,
    smoothing,
    grad_out,
):
    index = np.arange(HD) % (HD // 2)
    freq = jnp.asarray((10000.0 ** (-2.0 * index / HD)).astype(np.float32))[None, :]
    gh, gq, gkw, gvw, gks, gvs, gsm = finish(
        *main_call(
            hidden_states[0], positions, queries[0], key_weight, value_weight, key_step,
            value_step, smoothing[None, :], grad_out[0], freq,
        )
    )
    return gh[None], gq[None], gkw, gvw, gks, gvs, gsm.reshape(smoothing.shape)


def solution(mesh):
    in_specs = (
        P("dp", "ctx", None),
        P("dp", "ctx"),
        P("dp", "ctx", "tensor"),
        P("ctx", "tensor"),
        P("ctx", "tensor"),
        P("ctx", "tensor"),
        P("ctx", "tensor"),
        P(),
        P("dp", "ctx", "tensor"),
    )
    out_specs = (
        P("dp", "ctx", "tensor"),
        P("dp", "ctx", "tensor"),
        P("ctx", "tensor"),
        P("ctx", "tensor"),
        P("ctx", "tensor"),
        P("ctx", "tensor"),
        P(),
    )
    return jax.shard_map(body, mesh=mesh, in_specs=in_specs, out_specs=out_specs, check_vma=False)
```

```python
import functools
import math

import jax
import jax.numpy as jnp
import numpy as np
from jax import lax
from jax.experimental import pallas as pl
from jax.experimental.pallas import tpu as pltpu
from jax.sharding import PartitionSpec as P

HD = 128
GROUP = 128
TWO_PI = 2.0 * math.pi
LOG2E = 1.4426950408889634
SCALE = HD ** (-0.5)
MESH = pl.DeviceIdType.MESH
BF = jnp.bfloat16
F32 = jnp.float32
ANY = pl.BlockSpec(memory_space=pl.ANY)
DMA = pltpu.SemaphoreType.DMA
ZOFFSETS = (4, 3, -3, 2, -2, 1, -1)
VPEERS = ((2, 1), (1, 1), (3, 1), (2, 0), (1, 0), (3, 0), (0, 1))


class Place:
    def __init__(self):
        self.ctx = lax.axis_index("ctx")
        self.dp = lax.axis_index("dp")
        self.y = lax.axis_index("tensor")
        self.x = lax.div(self.ctx, 4)
        self.zl = lax.rem(self.ctx, 4)
        self.zh = lax.div(self.dp, 2)
        self.c = lax.rem(self.dp, 2)
        self.z = self.zh * 4 + self.zl

        self.X = [self.x] + [lax.rem(self.x + d, 4) for d in (1, 2, 3)]
        self.L = [self.zl] + [lax.rem(self.zl + d, 4) for d in (1, 2, 3)]
        self.Y = [self.y] + [lax.rem(self.y + d, 4) for d in (1, 2, 3)]
        self.Z = {}
        for d in (1, -1, 2, -2, 3, -3, 4):
            z = lax.rem(self.z + (d + 8), 8)
            self.Z[d] = (self.x * 4 + self.L[d % 4], lax.div(z, 4) * 2 + self.c)
        self.sibling = self.zh * 2 + (1 - self.c)

    def xn(self, d):
        return {"ctx": self.X[d % 4] * 4 + self.zl, "dp": self.dp}

    def zn(self, d):
        return {"ctx": self.Z[d][0], "dp": self.Z[d][1]}

    def at(self, dx, k):
        return {"ctx": self.X[dx % 4] * 4 + self.L[k % 4], "dp": self.dp}

    def zline(self, d):
        return {"ctx": self.x * 4 + self.L[d], "dp": self.dp}

    def yn(self, d):
        return {"tensor": self.Y[d % 4]}

    def ys(self, k, other):
        return {"tensor": self.Y[k], "dp": self.sibling if other else self.dp}

    def sib(self):
        return {"dp": self.sibling}

    def far(self, other):
        c = (1 - self.c) if other else self.c
        return {"dp": (1 - self.zh) * 2 + c}

    def mix(self, first, second, c):
        return {k: first[k] * (1 - c) + second[k] * c for k in first}


class Sender:
    def __init__(self, sems):
        self.sems = sems
        self.used = 0
        self.sent = []

    def make(self, index, what):
        src, dst, recv, peer = what()
        return pltpu.make_async_remote_copy(
            src_ref=src,
            dst_ref=dst,
            send_sem=self.sems.at[index],
            recv_sem=recv,
            device_id=peer,
            device_id_type=MESH,
        )

    def __call__(self, what):
        index = self.used
        self.used += 1
        self.sent.append((index, what))
        self.make(index, what).start()

    def drain(self):
        for index, what in self.sent:
            self.make(index, what).wait_send()
        self.sent = []


def arrived(ref, sem):
    pltpu.make_async_copy(ref, ref, sem).wait()


def sin_cos_turns(r):
    t = (r - jnp.floor(r + 0.5)) * TWO_PI
    q = t * t
    s = jnp.full_like(t, 1.0)
    for n in (14, 12, 10, 8, 6, 4, 2):
        s = 1.0 - q * s * (1.0 / (n * (n + 1)))
    k = jnp.full_like(t, 1.0)
    for n in (15, 13, 11, 9, 7, 5, 3, 1):
        k = 1.0 - q * k * (1.0 / (n * (n + 1)))
    return s * t, k


def spread(row):
    return jnp.broadcast_to(row, (128, row.shape[1])).T


def main_kernel(
    hid_h, pos_h, q_h, kw_h, vw_h, ks_h, vs_h, smooth_h, do_h, freq_h,
    gh_o, gq_o, gkw_o, gvw_o, gks_o, gvs_o, gsm_o,
    hid, pos, queries, kw, vw, ks, vs, smooth, dout, freq,
    cos, sin, inv, ss, st, cb,
    wbuf, sm, smt, smf, acc, kv, gall,
    qr, qt, do, dot_t, scr, dpr, dq, stm, stl, stu,
    a_st, a_rb, a_t, a_zs, a_z,
    wg, hs, hr, fs, fr, fb,
    y_s, y_r1, y_r2, yv, gs,
    dcol, gq, gkw, gvw, gks, gvs, gsm,
    ssem, csem, osem, nsem, sibsem, kvsem, gsem, tsem, tysem, asem, asend, azsem,
    fsem, y1sem, y2sem, vsem, gxsem, gzsem,
):
    p = Place()
    c = p.c
    pairs = (
        (kw_h, kw), (vw_h, vw), (ks_h, ks), (vs_h, vs), (smooth_h, smooth),
        (pos_h, pos), (freq_h, freq), (hid_h, hid), (q_h, queries), (do_h, dout),
    )
    loads = [pltpu.make_async_copy(s, d, csem.at[i]) for i, (s, d) in enumerate(pairs)]
    for load in loads:
        load.start()
    xr, xl, yr, yl, sib = p.xn(1), p.xn(-1), p.yn(1), p.yn(-1), p.sib()
    peers = [yr, yl, p.yn(2), sib] + [p.zn(k) for k in (1, -1, 2, -2, 3, -3, 4)]
    peers += [p.ys(k, 1) for k in (1, 2, 3)]
    peers += [p.at(dx, k) for dx in range(4) for k in range(4) if dx or k]
    barrier = pltpu.get_barrier_semaphore()
    for peer in peers:
        pl.semaphore_signal(barrier, inc=1, device_id=peer, device_id_type=MESH)
    send = Sender(ssem)

    slots = {}
    for a in range(4):
        for b in range(4):
            slots[a, b] = (p.X[a] * 4 + p.L[b]) * (1 - c) + (p.X[b] * 4 + p.L[a]) * c

    def slot(a, b):
        return slots[a % 4, b % 4]

    own = slot(0, 0)
    for load in loads[:5]:
        load.wait()

    def quantize(q):
        rows = pl.ds(pl.multiple_of(q * 128, 128), 128)
        s_row = smooth[:, pl.ds(pl.multiple_of(p.ctx * 512 + q * 128, 128), 128)]
        s_col = spread(s_row)
        for half, (w_ref, step_ref) in enumerate(((kw, ks), (vw, vs))):
            cols = slice(half * HD, (half + 1) * HD)
            weight = w_ref[rows, :].astype(F32)
            step = step_ref[pl.ds(q, 1), :]
            ratio = weight * s_col / step
            sine, cosine = sin_cos_turns(ratio)
            sine = sine * (1.0 / TWO_PI)
            quant = (step * (ratio - sine)).astype(BF)
            wbuf[own * 4 + q, :, cols] = quant
            slope = 1.0 - cosine
            ss[rows, cols] = slope * s_col
            st[rows, cols] = ratio * cosine - sine
            cb[rows, cols] = slope * weight - quant.astype(F32) / s_col

    quantize(c * 2)
    quantize(c * 2 + 1)
    pl.semaphore_wait(barrier, len(peers))

    an = {d: p.mix(p.xn(d), p.zn(d), c) for d in (1, -1)}
    bn = {d: p.mix(p.zn(d), p.xn(d), c) for d in (1, -1)}

    def chunk(s, sub):
        return wbuf.at[s * 4 + c * 2 + sub]

    def net(s, sub, peer):
        send(lambda: (chunk(s, sub), chunk(s, sub), nsem.at[s * 2 + sub], peer))

    def got(s, sub):
        arrived(chunk(s, sub), nsem.at[s * 2 + sub])

    def to_sib(s):
        ref = wbuf.at[pl.ds(s * 4 + c * 2, 2)]
        send(lambda: (ref, ref, sibsem.at[s], sib))

    def from_sib(s):
        arrived(wbuf.at[pl.ds(s * 4 + (1 - c) * 2, 2)], sibsem.at[s])

    def dot(s, h):
        w = wbuf[pl.ds(s * 4 + h * 2, 2)].reshape(256, 256)
        acc[...] += jnp.dot(sm[s * 2 + h], w, preferred_element_type=F32)

    for sub in (0, 1):
        net(own, sub, an[1])
        net(own, 1 - sub, an[-1])
        net(own, sub, bn[1])
        net(own, 1 - sub, bn[-1])

    def prepare(j0, j1):
        for j in range(j0, j1):
            cols = slice(j * 256, (j + 1) * 256)
            block = hid[:, cols].astype(F32) * inv[:, cols]
            sm[j] = block.astype(BF)

    inv[...] = 1.0 / smooth[...]
    left, right, far = slot(-1, 0), slot(1, 0), slot(2, 0)
    got(left, 0)
    net(left, 0, an[1])
    got(right, 1)
    net(right, 1, an[-1])
    for s, sub in ((left, 0), (right, 1)):
        net(s, sub, bn[1])
        net(s, sub, bn[-1])
    quantize((1 - c) * 2)
    quantize((1 - c) * 2 + 1)
    for s, sub in ((left, 1), (right, 0)):
        got(s, sub)
        net(s, sub, bn[1])
        net(s, sub, bn[-1])
        to_sib(s)
    loads[7].wait()
    prepare(0, 6)

    def across(a):
        bl, br = slot(a, -1), slot(a, 1)
        got(bl, 0)
        net(bl, 0, bn[1])
        got(br, 1)
        net(br, 1, bn[-1])
        got(bl, 1)
        got(br, 0)
        to_sib(bl)
        to_sib(br)
        return bl, br

    ready = [*across(0), left, right]
    for sub in (0, 1):
        got(far, sub)
        net(far, sub, bn[1])
        net(far, sub, bn[-1])
    to_sib(far)
    ready.append(far)
    prepare(6, 24)
    for load in loads[5:7]:
        load.wait()
    angle = spread(pos[...].astype(F32)) * freq[...]
    cos[...] = jnp.cos(angle)
    turned = jnp.sin(angle)
    lane = lax.broadcasted_iota(jnp.int32, (128, 128), 1)
    sin[...] = jnp.where(lane < HD // 2, -turned, turned)

    ready += across(-1)
    prepare(24, 32)
    groups = qr.shape[0] // 128
    for load in loads[8:]:
        load.wait()
    for g in range(groups):
        cols = slice(g * 128, (g + 1) * 128)
        q = queries[:, cols].astype(F32)
        q = q * cos[...] + pltpu.roll(q, HD // 2, 1) * sin[...]
        qr[cols, :] = q.astype(BF)
        qt[:, cols] = q.T.astype(BF)
        d = dout[:, cols]
        do[cols, :] = d
        dot_t[:, cols] = d.astype(F32).T.astype(BF)
    acc[...] = jnp.zeros_like(acc)
    dot(own, 0)
    dot(own, 1)
    ready += across(1)

    for s in ready[:5]:
        dot(s, c)
    ready += across(2)
    for s in ready[5:]:
        dot(s, c)
    for a in (-1, 1, 0, 2):
        for b in (0, -1, 1):
            if a == 0 and b == 0:
                continue
            s = slot(b, a)
            from_sib(s)
            dot(s, 1 - c)
    for a in (0, -1, 1, 2):
        s = slot(a, 2)
        got(s, 0)
        got(s, 1)
        to_sib(s)
        dot(s, c)
    for a in (-1, 1, 0, 2):
        s = slot(2, a)
        from_sib(s)
        dot(s, 1 - c)

    key_raw = acc[:, :HD]
    rotated = key_raw * cos[...] + pltpu.roll(key_raw, HD // 2, 1) * sin[...]
    kv[p.ctx, :, :HD] = rotated.astype(BF)
    kv[p.ctx, :, HD:] = acc[:, HD:].astype(BF)

    def kslot(d, k):
        return p.X[d % 4] * 4 + p.L[k % 4]

    def ksend(d, k, peer, buf=kv, sem=kvsem):
        def what():
            s = kslot(d, k)
            return buf.at[s], buf.at[s], sem.at[s], peer()

        send(what)

    def kgot(d, k, buf=kv, sem=kvsem):
        s = kslot(d, k)
        arrived(buf.at[s], sem.at[s])

    to_right, to_left = (lambda: p.xn(1)), (lambda: p.xn(-1))
    ksend(0, 0, to_right)
    ksend(0, 0, to_left)
    for k in (2, 1, 3):
        ksend(0, 0, functools.partial(p.zline, k))

    for j in range(32):
        smt[j * 2 : j * 2 + 2] = sm[j].astype(F32).T.astype(BF).reshape(2, 128, 128)
    smf[p.y, :, pl.ds(pl.multiple_of(p.ctx * 128, 128), 128)] = smt[p.ctx * 4 + p.y]
    width = 256
    chunks = qr.shape[0] // width
    q_index = p.ctx * 128 + lax.rem(lax.broadcasted_iota(jnp.int32, (1, width), 1), 128)
    first = q_index - jnp.concatenate([pos[...]] * (width // 128), axis=1)
    row = lax.broadcasted_iota(jnp.int32, (256, width), 0)
    def token_send(dx, k):
        def what():
            dest = p.X[dx] * 4 + p.L[k]
            cols = pl.ds(pl.multiple_of(p.ctx * 128, 128), 128)
            return smt.at[dest * 4 + p.y], smf.at[p.y, :, cols], tsem.at[p.ctx], p.at(dx, k)

        send(what)

    def fhalf(d, h):
        return smf.at[p.Y[d % 4], h * 64 : h * 64 + 64]

    def fsend(d, h, peer):
        send(
            lambda: (
                fhalf(d, h), fhalf(d, h), tysem.at[p.Y[d % 4], h], peer
            )
        )

    def fgot(d, h):
        arrived(fhalf(d, h), tysem.at[p.Y[d % 4], h])

    stm[...] = jnp.full_like(stm, -1e30)
    stl[...] = jnp.zeros_like(stl)
    stu[...] = jnp.zeros_like(stu)

    def stats(j):
        kj = kv[pl.ds(j * 2, 2), :, :HD].reshape(256, HD)
        vj = kv[pl.ds(j * 2, 2), :, HD:].reshape(256, HD)
        k_index = row + j * 256
        allowed = (k_index <= q_index) & (k_index >= first)
        for n in range(chunks):
            cols = slice(n * width, (n + 1) * width)
            m = stm[:, cols]
            s = jnp.dot(kj, qt[:, cols], preferred_element_type=F32) * (SCALE * LOG2E)
            s = jnp.where(allowed, s, -1e30)
            d = jnp.dot(vj, dot_t[:, cols], preferred_element_type=F32)
            scr[j, :, cols] = s
            dpr[j, :, cols] = d
            m_new = jnp.maximum(m, jnp.max(s, axis=0, keepdims=True))
            e = jnp.where(allowed, jnp.exp2(s - m_new), 0.0)
            fix = jnp.exp2(m - m_new)
            stm[:, cols] = m_new
            stl[:, cols] = stl[:, cols] * fix + jnp.sum(e, axis=0, keepdims=True)
            stu[:, cols] = stu[:, cols] * fix + jnp.sum(e * d, axis=0, keepdims=True)

    def group_step(g, _):
        @pl.when(g == 0)
        def _():
            for k in (1, 3, 2):
                kgot(0, k)
                ksend(0, k, to_right)
                ksend(0, k, to_left)

        @pl.when(g == 1)
        def _():
            for k in (0, 1, 3, 2):
                kgot(-1, k)
                if k in (0, 2):
                    ksend(-1, k, to_right)
                kgot(1, k)
                if k in (1, 3):
                    ksend(1, k, to_left)
            for dx in range(4):
                for k in range(4):
                    if dx or k:
                        token_send(dx, k)

        @pl.when(g == 3)
        def _():
            for k in (0, 1, 3, 2):
                kgot(2, k)

        d = g + lax.div(g, 2) - 2 * lax.div(g, 3)

        def pair_step(r, _):
            j = lax.rem(p.x + d, 4) * 2 + r

            @pl.when(j * 2 <= p.ctx)
            def _():
                stats(j)

            return 0

        return lax.fori_loop(0, 2, pair_step, 0)

    lax.fori_loop(0, 4, group_step, 0)

    shift = [stm[:, n * width : (n + 1) * width] for n in range(chunks)]
    delta = []
    for n in range(chunks):
        cols = slice(n * width, (n + 1) * width)
        shift[n] = shift[n] + jnp.log2(stl[:, cols])
        delta.append(stu[:, cols] / stl[:, cols])
    for n in range(chunks):
        cols = slice(n * width, (n + 1) * width)
        stm[:, cols] = shift[n]
        stu[:, cols] = delta[n]
    dq[...] = jnp.zeros_like(dq)

    def acopy(v, t):
        peer = p.mix(p.xn(1), p.xn(-1), lax.rem(t, 2))
        return pltpu.make_async_remote_copy(
            src_ref=a_st.at[v, t],
            dst_ref=a_rb.at[v, t],
            send_sem=asend.at[v, t],
            recv_sem=asem.at[v, t],
            device_id=peer,
            device_id_type=MESH,
        )

    def grads(t, _):
        q, r = lax.div(t, 2), lax.rem(t, 2)
        middle = lax.div(q * (3 - q), 2)
        d = middle * (1 + 2 * r) + (1 - middle) * lax.div((3 - q) * 2, 3)
        flip = middle * (2 - q)
        h = r + flip * (1 - 2 * r)
        j = lax.rem(p.x + d, 4) * 2 + h

        @pl.when(j * 2 <= p.ctx)
        def _():
            kj = kv[pl.ds(j * 2, 2), :, :HD].reshape(256, HD)
            kt = kj.astype(F32).T.astype(BF)
            dk = jnp.zeros((256, HD), F32)
            dv = jnp.zeros((256, HD), F32)
            for n in range(chunks):
                cols = slice(n * width, (n + 1) * width)
                prob = jnp.exp2(scr[j, :, cols] - stm[:, cols])
                ds = (prob * (dpr[j, :, cols] - stu[:, cols])).astype(BF)
                dv += jnp.dot(prob.astype(BF), do[cols, :], preferred_element_type=F32)
                dk += jnp.dot(ds, qr[cols, :], preferred_element_type=F32)
                dq[:, cols] += jnp.dot(kt, ds, preferred_element_type=F32)
            a_st[0, t] = (dk * SCALE).astype(BF).reshape(2, 128, HD)
            a_st[1, t] = dv.astype(BF).reshape(2, 128, HD)

        @pl.when(j * 2 > p.ctx)
        def _():
            a_st[0, t] = jnp.zeros((2, 128, HD), BF)
            a_st[1, t] = jnp.zeros((2, 128, HD), BF)

        @pl.when(t == 4)
        def _():
            for dx in range(4):
                for k in range(4):
                    if dx or k:
                        source = kslot(dx, k)
                        cols = pl.ds(pl.multiple_of(source * 128, 128), 128)
                        arrived(smf.at[p.y, :, cols], tsem.at[source])
            for h in (0, 1):
                fsend(0, h, yr)
                fsend(0, 1 - h, yl)

        @pl.when(q == 2)
        def _():
            for v in (0, 1):
                arrived(a_rb.at[v, t - 4], asem.at[v, t - 4])
                total = a_st[v, t].astype(F32) + a_rb[v, t - 4].astype(F32)
                a_st[v, t] = total.astype(BF)
                acopy(v, t).start()

        @pl.when(t < 4)
        def _():
            acopy(0, t).start()
            acopy(1, t).start()

        return 0

    lax.fori_loop(0, 8, grads, 0)

    for v in (0, 1):
        for t in (2, 3, 4, 5):
            arrived(a_rb.at[v, t], asem.at[v, t])
        for h, (near, run) in enumerate(((3, 4), (2, 5))):
            total = a_st[v, 6 + h].astype(F32) + a_rb[v, near].astype(F32)
            total = total + a_rb[v, run].astype(F32)
            a_t[v, h * 2 : h * 2 + 2] = total
            a_zs[v, h * 2 : h * 2 + 2] = total.astype(BF)
        for k in (2, 1, 3):
            send(
                functools.partial(
                    lambda v, k: (
                        a_zs.at[v, p.L[k % 4]], a_z.at[v, k - 1],
                        azsem.at[v, k - 1], p.zline(k),
                    ),
                    v, k,
                )
            )
    for g in range(groups):
        cols = slice(g * 128, (g + 1) * 128)
        t = dq[:, cols].T * SCALE
        gq[:, cols] = t * cos[...] - pltpu.roll(t, HD // 2, 1) * sin[...]
    stores = [pltpu.make_async_copy(gq, gq_o, osem.at[0])]
    stores[0].start()

    def gsend(v, d, k, peer):
        ksend(d, k, peer, gall.at[v], gsem.at[v])

    def ggot(v, d, k):
        kgot(d, k, gall.at[v], gsem.at[v])

    parts = []
    for v in (0, 1):
        total = a_t[v, p.zl]
        for k in (1, 3, 2):
            arrived(a_z.at[v, k - 1], azsem.at[v, k - 1])
            total += a_z[v, k - 1].astype(F32)
        if v == 0:
            total = total * cos[...] - pltpu.roll(total, HD // 2, 1) * sin[...]
        parts.append(total.astype(BF))
        gall[v, p.ctx] = parts[v]
        for k in (2, 1, 3):
            gsend(v, 0, 0, functools.partial(p.zline, k))
        gsend(v, 0, 0, to_right)
        gsend(v, 0, 0, to_left)
    g = jnp.concatenate(parts, axis=1)
    def dgrad(d, h):
        blk = p.Y[d % 4] * 16 + h * 8
        out = []
        for i in range(4):
            wb = wbuf[pl.ds(blk + i * 2, 2)].reshape(256, 256)
            out.append(
                lax.dot_general(g, wb, (((1,), (1,)), ((), ())), preferred_element_type=F32)
            )
        return out

    def dstore(k, d, h, extra=None):
        for i, piece in enumerate(dgrad(d, h)):
            cols = slice(i * 256, (i + 1) * 256)
            if extra is not None:
                piece = piece + extra[:, cols].astype(F32)
            y_s[k, h, :, cols] = piece.astype(BF)

    fgot(-1, 0)
    fsend(-1, 0, yr)
    fgot(1, 1)
    fsend(1, 1, yl)
    dstore(0, 2, 0)
    send(lambda: (y_s.at[0, 0], y_r1.at[0], y1sem.at[0], yr))
    dstore(0, 2, 1)
    send(lambda: (y_s.at[0, 1], y_r1.at[1], y1sem.at[1], yl))

    for v in (0, 1):
        for k in (1, 3, 2):
            ggot(v, 0, k)
            gsend(v, 0, k, to_right)
            gsend(v, 0, k, to_left)
    dstore(1, 1, 1)
    send(lambda: (y_s.at[1, 1], y_r2.at[0, 1], y2sem.at[1], yr))
    for a, b in ((0, 1), (2, 3)):
        if a == 0:
            dstore(2, -1, 0)
            send(lambda: (y_s.at[2, 0], y_r2.at[1, 0], y2sem.at[2], yl))
        for v in (0, 1):
            ggot(v, -1, a)
            gsend(v, -1, a, to_right)
            ggot(v, 1, b)
            gsend(v, 1, b, to_left)
    for d, h in ((-1, 1), (1, 0), (2, 0), (2, 1)):
        fgot(d, h)

    far_id = p.far(0)

    def fcopy(v):
        send(lambda: (fs.at[v], fr.at[v], fsem.at[v, 1], far_id))

    early = len(send.sent)
    vec = [jnp.zeros((1, 128), F32) for _ in range(4)]
    for v in (0, 1):
        for k in (1, 3):
            ggot(v, -1, k)
        for k in (0, 2):
            ggot(v, 1, k)
        for k in (0, 1, 3, 2):
            ggot(v, 2, k)
        tokens = gall[v].reshape(2048, HD)
        for half in (1 - c, c):
            for i in (0, 1):
                q = half * 2 + i
                rows = pl.ds(pl.multiple_of(q * 128, 128), 128)
                value = jnp.dot(smf[q], tokens, preferred_element_type=F32)
                wg[v, rows, :] = value
                if half is not c:
                    hs[v, i] = value.astype(BF)
            if half is not c:
                send(functools.partial(lambda v: (hs.at[v], hr.at[v], fsem.at[v, 0], sib), v))
        cols = slice(v * HD, (v + 1) * HD)
        for q in range(4):
            rows = slice(q * 128, (q + 1) * 128)
            vec[q] += jnp.sum((wg[v, rows, :] * cb[rows, cols]).T, axis=0, keepdims=True)
        if v == 1:
            yv[p.y * 2 + p.c] = jnp.concatenate(vec + vec, axis=0)
            for k, other in VPEERS:
                send(
                    functools.partial(
                        lambda k, other: (
                            yv.at[p.y * 2 + p.c], yv.at[p.y * 2 + p.c],
                            vsem.at[k * 2 + other], p.ys(k, other),
                        ),
                        k, other,
                    )
                )
        arrived(hr.at[v], fsem.at[v, 0])
        for i in (0, 1):
            rows = pl.ds(pl.multiple_of((c * 2 + i) * 128, 128), 128)
            fs[v, i] = (wg[v, rows, :] + hr[v, i].astype(F32)).astype(BF)
        fcopy(v)

    arrived(y_r1.at[0], y1sem.at[0])
    dstore(1, 1, 0, y_r1.at[0])
    send(lambda: (y_s.at[1, 0], y_r2.at[0, 0], y2sem.at[0], yr))
    arrived(y_r1.at[1], y1sem.at[1])
    dstore(2, -1, 1, y_r1.at[1])
    send(lambda: (y_s.at[2, 1], y_r2.at[1, 1], y2sem.at[3], yl))

    late = send.sent[early:]
    send.sent = send.sent[:early]
    for k, other in VPEERS:
        core = c * (1 - other) + (1 - c) * other
        arrived(yv.at[p.Y[(4 - k) % 4] * 2 + core], vsem.at[k * 2 + other])
    first_sent, send.sent = send.sent, []
    gs[p.z, p.x] = ((yv[0] + yv[1]) + (yv[2] + yv[3])) + ((yv[4] + yv[5]) + (yv[6] + yv[7]))
    for k in (2, 1, 3):
        send(
            functools.partial(
                lambda k: (gs.at[p.z, p.x], gs.at[p.z, p.x], gxsem.at[k - 1], p.xn(k)), k
            )
        )

    for k in (1, 3, 2):
        arrived(gs.at[p.z, p.X[4 - k]], gxsem.at[k - 1])
    for k in ZOFFSETS:
        send(
            functools.partial(
                lambda k: (gs.at[p.z], gs.at[p.z], gzsem.at[k + 3], p.zn(k)), k
            )
        )
    tail, send.sent = send.sent, first_sent
    send.drain()
    for v in (0, 1):
        for t in range(6):
            acopy(v, t).wait_send()
    send.sent = late + tail
    for v in (0, 1):
        arrived(fr.at[v], fsem.at[v, 1])
        fb[v, pl.ds(c * 2, 2)] = (fs[v].astype(F32) + fr[v].astype(F32)).astype(BF)
        send(
            functools.partial(
                lambda v: (
                    fb.at[v, pl.ds(c * 2, 2)], fb.at[v, pl.ds(c * 2, 2)], fsem.at[v, 2], sib
                ),
                v,
            )
        )
    inv_cols = inv[:, pl.ds(pl.multiple_of(p.y * 2048, 2048), 2048)]
    for h in (0, 1):
        for i, piece in enumerate(dgrad(0, h)):
            dcol[:, h * 1024 + i * 256 : h * 1024 + (i + 1) * 256] = piece
    for i, (s, h) in ((1, (0, 1)), (2, (1, 0)), (0, (0, 0)), (3, (1, 1))):
        arrived(y_r2.at[s, h], y2sem.at[i])
    for h in (0, 1):
        cols = slice(h * 1024, (h + 1) * 1024)
        total = dcol[:, cols] + y_r2[0, h].astype(F32) + y_r2[1, h].astype(F32)
        dcol[:, cols] = total * inv_cols[:, cols]
    stores.append(pltpu.make_async_copy(dcol, gh_o, osem.at[1]))
    stores[-1].start()

    for v, (weights, totals) in enumerate(((gkw, gks), (gvw, gvs))):
        arrived(fb.at[v, pl.ds((1 - c) * 2, 2)], fsem.at[v, 2])
        cols = slice(v * HD, (v + 1) * HD)
        for q in range(4):
            rows = slice(q * 128, (q + 1) * 128)
            f = fb[v, q].astype(F32)
            weights[rows, :] = f * ss[rows, cols]
            totals[q : q + 1, :] = jnp.sum(f * st[rows, cols], axis=0, keepdims=True)
    for i, (src, dst) in enumerate(((gkw, gkw_o), (gvw, gvw_o), (gks, gks_o), (gvs, gvs_o))):
        stores.append(pltpu.make_async_copy(src, dst, osem.at[2 + i]))
        stores[-1].start()

    for k in ZOFFSETS:
        arrived(gs.at[lax.rem(p.z + (8 - k), 8)], gzsem.at[k + 3])
    for i in range(16):
        zl, x = i % 4, i // 4
        gsm[i * 4 : i * 4 + 4, :] = gs[zl, x, :4, :] + gs[4 + zl, x, :4, :]
    stores.append(pltpu.make_async_copy(gsm, gsm_o, osem.at[6]))
    stores[-1].start()

    send.drain()
    for store in stores:
        store.wait()


def main_call(*args):
    rows = args[2].shape[1]
    outs = (
        ((128, 2048), F32), ((128, rows), F32), ((512, 128), F32), ((512, 128), F32),
        ((4, 128), F32), ((4, 128), F32), ((64, 128), F32),
    )
    scratch = [pltpu.VMEM(a.shape, a.dtype) for a in args]
    scratch += [pltpu.VMEM(*s) for s in (
        ((128, 128), F32), ((128, 128), F32), ((1, 8192), F32),
        ((512, 256), F32), ((512, 256), F32), ((512, 256), F32),
        ((64, 128, 256), BF), ((32, 128, 256), BF), ((64, 128, 128), BF),
        ((4, 128, 2048), BF), ((128, 256), F32), ((16, 128, 256), BF), ((2, 16, 128, 128), BF),
        ((rows, HD), BF), ((HD, rows), BF), ((rows, HD), BF), ((HD, rows), BF),
        ((8, 256, rows), F32), ((8, 256, rows), F32), ((HD, rows), F32),
        ((1, rows), F32), ((1, rows), F32), ((1, rows), F32),
        ((2, 8, 2, 128, 128), BF), ((2, 6, 2, 128, 128), BF), ((2, 4, 128, 128), F32),
        ((2, 4, 128, 128), BF), ((2, 3, 128, 128), BF),
        ((2, 512, 128), F32), ((2, 2, 128, 128), BF), ((2, 2, 128, 128), BF),
        ((2, 2, 128, 128), BF), ((2, 2, 128, 128), BF), ((2, 4, 128, 128), BF),
        ((3, 2, 128, 1024), BF), ((2, 128, 1024), BF), ((2, 2, 128, 1024), BF),
        ((8, 8, 128), F32), ((8, 4, 8, 128), F32),
    )]
    scratch += [pltpu.VMEM(*o) for o in outs]
    scratch += [DMA(s) for s in (
        (192,), (10,), (7,), (32,), (16,), (16,), (2, 16), (16,), (4, 2), (2, 6), (2, 6),
        (2, 3), (2, 3), (2,), (4,), (8,), (3,), (8,),
    )]
    return pl.pallas_call(
        main_kernel,
        name="main",
        out_shape=tuple(jax.ShapeDtypeStruct(*o) for o in outs),
        in_specs=[ANY] * len(args),
        out_specs=(ANY,) * len(outs),
        scratch_shapes=scratch,
        compiler_params=pltpu.CompilerParams(
            collective_id=0, has_side_effects=True, vmem_limit_bytes=60 << 20
        ),
    )(*args)


def finish_kernel(*refs):
    count = (len(refs) - 1) // 3
    sems = refs[-1]
    loads, stores = [], []
    for i in range(count):
        held = refs[2 * count + i]
        loads.append(pltpu.make_async_copy(refs[i], held, sems.at[0, i]))
        stores.append(pltpu.make_async_copy(held, refs[count + i], sems.at[1, i]))
    for load in loads:
        load.start()
    for load, store in zip(loads, stores):
        load.wait()
        store.start()
    for store in stores:
        store.wait()


def finish(*arrays):
    return pl.pallas_call(
        finish_kernel,
        name="finish",
        out_shape=tuple(jax.ShapeDtypeStruct(a.shape, a.dtype) for a in arrays),
        in_specs=[ANY] * len(arrays),
        out_specs=(ANY,) * len(arrays),
        scratch_shapes=[pltpu.VMEM(a.shape, a.dtype) for a in arrays] + [DMA((2, len(arrays)))],
        compiler_params=pltpu.CompilerParams(vmem_limit_bytes=60 << 20),
    )(*arrays)


def body(
    hidden_states,
    positions,
    queries,
    key_weight,
    value_weight,
    key_step,
    value_step,
    smoothing,
    grad_out,
):
    index = np.arange(HD) % (HD // 2)
    freq = jnp.asarray((10000.0 ** (-2.0 * index / HD)).astype(np.float32))[None, :]
    gh, gq, gkw, gvw, gks, gvs, gsm = finish(
        *main_call(
            hidden_states[0], positions, queries[0], key_weight, value_weight, key_step,
            value_step, smoothing[None, :], grad_out[0], freq,
        )
    )
    return gh[None], gq[None], gkw, gvw, gks, gvs, gsm.reshape(smoothing.shape)


def solution(mesh):
    in_specs = (
        P("dp", "ctx", None),
        P("dp", "ctx"),
        P("dp", "ctx", "tensor"),
        P("ctx", "tensor"),
        P("ctx", "tensor"),
        P("ctx", "tensor"),
        P("ctx", "tensor"),
        P(),
        P("dp", "ctx", "tensor"),
    )
    out_specs = (
        P("dp", "ctx", "tensor"),
        P("dp", "ctx", "tensor"),
        P("ctx", "tensor"),
        P("ctx", "tensor"),
        P("ctx", "tensor"),
        P("ctx", "tensor"),
        P(),
    )
    return jax.shard_map(body, mesh=mesh, in_specs=in_specs, out_specs=out_specs, check_vma=False)
```
